128 devices in a mesh: seq: 64 (over y, x, z), tp: 2 (over core).
Axes of the slice: x: 4, y: 4, z: 4, core: 2. Of those that a mesh axis runs over, the one named last changes fastest.
Arguments:
- tokens: bfloat16 [8192, 2048], P('seq'), may hold values from -16 to 16
- mixer_gain: float32 [2048], replicated, may hold values from 0.5 to 1.5
- mixer_bias: float32 [2048], replicated, may hold values from -1.75 to 1.75
- query_weight: bfloat16 [2048, 2048], P('seq', 'tp'), may hold values from -0.125 to 0.125
- key_weight: bfloat16 [2048, 2048], P('seq', 'tp'), may hold values from -0.125 to 0.125
- value_weight: bfloat16 [2048, 4096], P('seq', 'tp'), may hold values from -0.125 to 0.125
- swish_weight: bfloat16 [2048, 4096], P('seq', 'tp'), may hold values from -0.125 to 0.125
- output_weight: bfloat16 [2048, 4096], P('seq', 'tp'), may hold values from -0.1875 to 0.1875
- feed_gain: float32 [2048], replicated, may hold values from 0.5 to 1.5
- feed_bias: float32 [2048], replicated, may hold values from -1.75 to 1.75
- gate_weight: bfloat16 [2048, 4096], P('seq', 'tp'), may hold values from -0.125 to 0.125
- up_weight: bfloat16 [2048, 4096], P('seq', 'tp'), may hold values from -0.125 to 0.125
- down_weight: bfloat16 [2048, 4096], P('seq', 'tp'), may hold values from -0.1875 to 0.1875
- cotangent: bfloat16 [8192, 2048], P('seq'), may hold values from -16 to 16
Outputs:
- block_output: bfloat16 [8192, 2048], P('seq')
- tokens_grad: float32 [8192, 2048], P('seq')
- mixer_gain_grad: float32 [2048], P('seq')
- mixer_bias_grad: float32 [2048], P('seq')
- query_grad: float32 [2048, 2048], P('seq', 'tp')
- key_grad: float32 [2048, 2048], P('seq', 'tp')
- value_grad: float32 [2048, 4096], P('seq', 'tp')
- swish_grad: float32 [2048, 4096], P('seq', 'tp')
- output_grad: float32 [2048, 4096], P('seq', 'tp')
- feed_gain_grad: float32 [2048], P('seq')
- feed_bias_grad: float32 [2048], P('seq')
- gate_grad: float32 [2048, 4096], P('seq', 'tp')
- up_grad: float32 [2048, 4096], P('seq', 'tp')
- down_grad: float32 [2048, 4096], P('seq', 'tp')
The draws below stay inside these ranges and needn't reach their ends.
All inputs are finite; a program needn't handle non-finite values.
Results may differ from the reference program's by a relative error of at most 0.0141.
Values may be sent and summed in bfloat16 or wider, within the bound.
No kernel may reach another device: no remote copies, remote signals or barrier semaphores. Data moves between devices by JAX's collectives and lax.ppermute only.
A program may use at most 576 MiB of HBM per device.

```python
import jax
import jax.numpy as jnp
from jax import lax

D = 2048
HEADS = 8
DK = 256
DV = 512
FF = 4096
TOK_DEV = 128
TOKENS = 8192


def spiked(values, key, source, target, shards_of, factor):
    owner, partner = [(jnp.arange(values.shape[axis_at]) // (values.shape[axis_at] // shards_of)).reshape([-1 if axis == axis_at else 1 for axis in range(values.ndim)]) for axis_at in (source, target)]
    chosen = jax.random.permutation(key, shards_of)[partner]
    strong = (owner == chosen) | (owner == (partner + shards_of // 2) % shards_of)
    return jnp.where(strong, factor * values, values)


def steps_of(stream_key, dims, cuts, low, high):
    loudness, own = 1.0, jax.random.fold_in(stream_key, 6)
    for dim, shards_of in cuts:
        steps = jnp.exp(jax.random.uniform(jax.random.fold_in(own, dim), (shards_of,), jnp.float32, low / len(cuts), high / len(cuts)))
        loudness = loudness * jnp.repeat(steps, dims[dim] // shards_of).reshape([-1 if axis == dim else 1 for axis in range(len(dims))])
    return loudness


def bell_draw(own_key, shape, scale, bound, shards=(), held_as=jnp.bfloat16):
    array = scale * jax.random.normal(own_key, shape, jnp.float32)
    if shards:
        array = array * steps_of(own_key, shape, shards, -0.22, 0.18)
    return jnp.clip(array, -bound, bound).astype(held_as)


def heavy_noise(rng, dims, spread, reach, split, heavy, kind=jnp.bfloat16):
    array = spread * jax.random.normal(rng, dims, jnp.float32)
    if split:
        array = array * steps_of(rng, dims, split, -0.22, 0.18)
    return jnp.clip(spiked(array, jax.random.fold_in(rng, 3), *heavy), -reach, reach).astype(kind)


def setup_inputs(seed: int = 0) -> dict:
    key_list = jax.random.split(jax.random.key(seed), 15)
    return {
        "tokens": heavy_noise(key_list[0], (TOKENS, D), 1.0, 16.0, ((0, 64),), (0, 1, 64, 4.0)),
        "mixer_gain": jnp.clip(1.0 + 0.1 * jax.random.normal(key_list[1], (D,), jnp.float32), 0.5, 1.5),
        "mixer_bias": bell_draw(key_list[2], (D,), 0.3, 1.75, (), jnp.float32),
        "query_weight": bell_draw(key_list[3], (D, HEADS * DK), D ** -0.5, 0.125, ((0, 64), (1, 2))),
        "key_weight": bell_draw(key_list[4], (D, HEADS * DK), D ** -0.5, 0.125, ((0, 64), (1, 2))),
        "value_weight": bell_draw(key_list[5], (D, HEADS * DV), D ** -0.5, 0.125, ((0, 64), (1, 2))),
        "swish_weight": bell_draw(key_list[6], (D, HEADS * DV), D ** -0.5, 0.125, ((0, 64), (1, 2))),
        "output_weight": bell_draw(key_list[7], (D, HEADS * DV), (HEADS * DV // 4) ** -0.5, 0.1875, ((0, 64), (1, 2))),
        "feed_gain": jnp.clip(1.0 + 0.1 * jax.random.normal(key_list[8], (D,), jnp.float32), 0.5, 1.5),
        "feed_bias": bell_draw(key_list[9], (D,), 0.3, 1.75, (), jnp.float32),
        "gate_weight": bell_draw(key_list[10], (D, FF), D ** -0.5, 0.125, ((0, 64), (1, 2))),
        "up_weight": bell_draw(key_list[11], (D, FF), D ** -0.5, 0.125, ((0, 64), (1, 2))),
        "down_weight": bell_draw(key_list[12], (D, FF), (FF // 4) ** -0.5, 0.1875, ((0, 64), (1, 2))),
        "cotangent": heavy_noise(key_list[13], (TOKENS, D), 1.0, 16.0, ((0, 64),), (0, 1, 64, 4.0)),
    }


@jax.custom_vjp
def low(v):
    return lax.optimization_barrier(v.astype(jnp.bfloat16)).astype(jnp.float32)

@jax.custom_vjp
def low_back(v):
    return v

def low_keep(v):
    return (low(v), None)

def low_pass(kept, grad):
    return (grad,)

def back_keep(v):
    return (v, None)

def back_low(kept, grad):
    return (low(grad),)
low.defvjp(low_keep, low_pass)
low_back.defvjp(back_keep, back_low)

def product(left_side, right_side):
    return jnp.dot(left_side, right_side, precision=lax.Precision.HIGHEST, preferred_element_type=jnp.float32)

def layer_norm(values, gain, bias):
    centred = values - lax.optimization_barrier(jnp.mean(values, axis=-1, keepdims=True))
    return centred * lax.rsqrt(lax.optimization_barrier(jnp.mean(centred * centred, axis=-1, keepdims=True)) + 1e-05) * gain + bias

def group_norm(values):
    centred = values - lax.optimization_barrier(jnp.mean(values, axis=-1, keepdims=True))
    return centred * lax.rsqrt(lax.optimization_barrier(jnp.mean(centred * centred, axis=-1, keepdims=True)) + 1e-05)

def angles(positions):
    frequency = 1.0 / 10000.0 ** jnp.linspace(0.0, 1.0, DK // 2, dtype=jnp.float32)
    phases = positions[:, None] * frequency[None, :]
    return (jnp.cos(phases)[:, None, :], jnp.sin(phases)[:, None, :])

def rotate_pairs(values, cosine, sinewave):
    paired = values.reshape(values.shape[:-1] + (values.shape[-1] // 2, 2))
    leading = paired[..., 0]
    trailing = paired[..., 1]
    turned = jnp.stack([leading * cosine - trailing * sinewave, trailing * cosine + leading * sinewave], axis=-1)
    return turned.reshape(values.shape)

def retention(queries_in, keys_in, values_in):
    highest = lax.Precision.HIGHEST
    decay_rates = jnp.log(1.0 - 2.0 ** (-5.0 - jnp.arange(HEADS, dtype=jnp.float32)))
    blocksize = TOK_DEV
    places = jnp.arange(blocksize, dtype=jnp.float32)
    offsets = places[:, None] - places[None, :]
    within = jnp.where(offsets[None] >= 0, jnp.exp(jnp.maximum(offsets, 0.0)[None] * decay_rates[:, None, None]), 0.0)
    onward = jnp.exp(places[:, None] * decay_rates[None, :])
    leftover = jnp.exp((blocksize - places)[:, None] * decay_rates[None, :])
    carry_decay = jnp.exp(blocksize * decay_rates)

    def advance(carried, triple):
        query_block, key_block, value_block = triple
        scores = jnp.einsum('ihd,jhd->hij', query_block, key_block, precision=highest) * within
        local_part = jnp.einsum('hij,jhe->ihe', scores, value_block, precision=highest)
        carried_part = jnp.einsum('ihd,hde->ihe', query_block, carried, precision=highest) * onward[:, :, None]
        update = jnp.einsum('jhd,jhe->hde', key_block * leftover[:, :, None], value_block, precision=highest)
        return (carry_decay[:, None, None] * carried + update, local_part + carried_part)
    blocks = TOKENS // blocksize
    pieces = (queries_in.reshape(blocks, blocksize, HEADS, DK), keys_in.reshape(blocks, blocksize, HEADS, DK), values_in.reshape(blocks, blocksize, HEADS, DV))
    initial = jnp.zeros((HEADS, DK, DV), jnp.float32)
    last_state, outputs = lax.scan(jax.checkpoint(advance), initial, pieces)
    return outputs.reshape(TOKENS, HEADS, DV)

def forward(residual_in, mixer_gain, mixer_bias, query_weight, key_weight, value_weight, swish_weight, output_weight, feed_gain, feed_bias, gate_weight, up_weight, down_weight):
    normed = low(layer_norm(residual_in, mixer_gain, mixer_bias))
    queries = low_back(product(normed, query_weight)).reshape(TOKENS, HEADS, DK)
    keys_raw = low_back(product(normed, key_weight)).reshape(TOKENS, HEADS, DK)
    values = low(low_back(product(normed, value_weight))).reshape(TOKENS, HEADS, DV)
    switch = low_back(product(normed, swish_weight))
    cosine, sinewave = angles(jnp.arange(TOKENS, dtype=jnp.float32))
    turned_query = low(rotate_pairs(queries, cosine, sinewave))
    turned_key = low(rotate_pairs(keys_raw, cosine, sinewave) * DK ** (-0.5))
    retained = low_back(retention(turned_query, turned_key, values))
    scaled = group_norm(retained).reshape(TOKENS, HEADS * DV)
    branch = low(jax.nn.silu(switch) * scaled)
    attended = low_back(product(branch, output_weight.T))
    residual = residual_in + attended
    normed_two = low(layer_norm(residual, feed_gain, feed_bias))
    gate_pre = low_back(product(normed_two, gate_weight))
    upward = low_back(product(normed_two, up_weight))
    inner_act = low(jax.nn.silu(gate_pre) * upward)
    return residual + low_back(product(inner_act, down_weight.T))

def reference(tokens, mixer_gain, mixer_bias, query_weight, key_weight, value_weight, swish_weight, output_weight, feed_gain, feed_bias, gate_weight, up_weight, down_weight, cotangent):
    result, pullback = jax.vjp(forward, tokens.astype(jnp.float32), mixer_gain.astype(jnp.float32), mixer_bias.astype(jnp.float32), query_weight.astype(jnp.float32), key_weight.astype(jnp.float32), value_weight.astype(jnp.float32), swish_weight.astype(jnp.float32), output_weight.astype(jnp.float32), feed_gain.astype(jnp.float32), feed_bias.astype(jnp.float32), gate_weight.astype(jnp.float32), up_weight.astype(jnp.float32), down_weight.astype(jnp.float32))
    gradient_list = pullback(cotangent.astype(jnp.float32))
    return (result.astype(jnp.bfloat16), gradient_list[0], gradient_list[1], gradient_list[2], gradient_list[3], gradient_list[4], gradient_list[5], gradient_list[6], gradient_list[7], gradient_list[8], gradient_list[9], gradient_list[10], gradient_list[11], gradient_list[12])
```

```python
import jax
import jax.numpy as jnp
from jax import lax
from jax.sharding import PartitionSpec as P

DK = 256
DV = 512
SIDE = 4
BF = jnp.bfloat16
F32 = jnp.float32
STRIDE = {"y": 16, "x": 4, "z": 1}


def pairs(axis, step):
    table = []
    for source in range(64):
        place = source // STRIDE[axis] % SIDE
        target = source + ((place - step) % SIDE - place) * STRIDE[axis]
        table.append((source, target))
    return table


def hop(value, axis, step):
    return lax.ppermute(value, "seq", pairs(axis, step % SIDE))


def swap(value):
    return lax.ppermute(value, "tp", [(0, 1), (1, 0)])


def direct(value, axis):
    return [value] + [hop(value, axis, step) for step in (1, 2, 3)]


def relay(value, axis):
    half = value.shape[0] // 2
    ahead = hop(value, axis, 1)
    behind = hop(value, axis, 3)
    first = hop(ahead[:half], axis, 1)
    second = hop(behind[half:], axis, 3)
    return [value, ahead, jnp.concatenate([first, second], axis=0), behind]


def placed(pieces, start, axis):
    shape = pieces[0].shape[:axis] + (SIDE,) + pieces[0].shape[axis:]
    whole = jnp.zeros(shape, pieces[0].dtype)
    for step, piece in enumerate(pieces):
        whole = lax.dynamic_update_index_in_dim(whole, piece, (start + step) % SIDE, axis)
    return whole


def block(values, index):
    return lax.dynamic_index_in_dim(values, index % SIDE, 0, keepdims=False)


def exchange(packed, z):
    pieces = [block(packed, z)] + [hop(block(packed, z - step), "z", step) for step in (1, 2, 3)]
    return placed(pieces, z, 0)


def spread(part, first, second, where):
    columns = part.shape[-1]
    line = placed(direct(part, first), where[first], 0)
    pieces = relay(line.reshape(SIDE * part.shape[0], columns), second)
    pieces = [piece.reshape(SIDE, part.shape[0], columns) for piece in pieces]
    return placed(pieces, where[second], 0 if second == "y" else 1).reshape(-1, columns)


def gather_rows(rows):
    mine = jnp.concatenate(direct(rows, "z"), axis=0)
    return jnp.concatenate([mine, swap(mine)], axis=0)


def reduce_rows(part):
    part = part.reshape(2, SIDE, -1, part.shape[-1])
    pair = part[0] + swap(part[1].astype(BF)).astype(F32)
    total = pair[0]
    for step in (1, 2, 3):
        total = total + hop(pair[step].astype(BF), "z", -step).astype(F32)
    return total


def layer_stats(values):
    centred = values - jnp.mean(values, axis=-1, keepdims=True)
    scaling = lax.rsqrt(jnp.mean(centred * centred, axis=-1, keepdims=True) + 1e-05)
    return (centred * scaling, scaling)


def norm_back(grad_hat, normal, scaling):
    return scaling * (
        grad_hat
        - jnp.mean(grad_hat, axis=-1, keepdims=True)
        - normal * jnp.mean(grad_hat * normal, axis=-1, keepdims=True)
    )


def silu_slope(values):
    logistic = jax.nn.sigmoid(values)
    return logistic * (1.0 + values * (1.0 - logistic))


def mm(left, right, left_dim=1, right_dim=0):
    return lax.dot_general(
        left, right, (((left_dim,), (right_dim,)), ((), ())), preferred_element_type=F32
    )


def prefix(update, carry, where, backward):
    x, y = where["x"], where["y"]
    if backward:
        x, y = SIDE - 1 - x, SIDE - 1 - y
    sign = -1 if backward else 1
    power = lambda n: carry ** n.astype(F32)
    row = carry**4
    half = update.shape[1] // 2

    def other(mine, step):
        return (mine + sign * step) % SIDE

    left = update[:, :half]
    sent = left.astype(BF)
    inner, total = jnp.zeros_like(left), left * power(3 - x)
    for step in (1, 2, 3):
        got = hop(sent, "x", step).astype(F32)
        place = other(x, step)
        inner = inner + got * jnp.where(place < x, power(jnp.maximum(x - 1 - place, 0)), 0.0)
        total = total + got * power(3 - place)
    sent = total.astype(BF)
    outer = jnp.zeros_like(left)
    for step in (1, 2, 3):
        got = hop(sent, "y", step).astype(F32)
        place = other(y, step)
        outer = outer + got * jnp.where(place < y, row ** jnp.maximum(y - 1 - place, 0).astype(F32), 0.0)
    first = inner + outer * power(x)
    right = update[:, half:]
    sent = right.astype(BF)
    above = jnp.zeros_like(right)
    for step in (1, 2, 3):
        got = hop(sent, "y", step).astype(F32)
        place = other(y, step)
        above = above + got * jnp.where(place < y, row ** jnp.maximum(y - 1 - place, 0).astype(F32), 0.0)
    through = above * row + right
    second = above * power(jnp.full_like(x, 3))
    for step in (1, 2, 3):
        target = other(x, -step)
        got = hop(jnp.where(x < target, through, above).astype(BF), "x", step).astype(F32)
        place = other(x, step)
        second = second + got * power(jnp.where(place < x, x - 1 - place, x + 3 - place))
    return jnp.concatenate([first, second], axis=1)


def local(
    tokens,
    mixer_gain,
    mixer_bias,
    query_weight,
    key_weight,
    value_weight,
    swish_weight,
    output_weight,
    feed_gain,
    feed_bias,
    gate_weight,
    up_weight,
    down_weight,
    cotangent,
):
    place = lax.axis_index("seq")
    where = {"y": place // 16, "x": place // 4 % 4, "z": place % 4}
    z, t = where["z"], lax.axis_index("tp")
    rows = tokens.shape[0]
    half = rows // 2
    shard = query_weight.shape[0]
    planes = [[16 * b + 4 * a + c for b in range(4) for a in range(4)] for c in range(4)]

    column = jnp.arange(DK)
    order = jnp.where(column < DK // 2, 2 * column, 2 * column - DK + 1)
    shuffle = (jnp.arange(DK)[:, None] == order[None, :]).astype(BF)

    def heads(weight):
        return weight.reshape(shard, SIDE, -1)

    def split_pairs(weight):
        return mm(weight.reshape(shard * SIDE, DK), shuffle).astype(BF).reshape(shard, SIDE, DK)

    def packed(*weights):
        return jnp.concatenate(weights, axis=-1).transpose(1, 0, 2)

    def own(values):
        return lax.dynamic_slice_in_dim(values, t * half, half, 0)

    retention_share = exchange(
        packed(split_pairs(query_weight), split_pairs(key_weight), heads(value_weight)), z
    ).reshape(rows, -1)
    feed_share = exchange(
        packed(heads(gate_weight), heads(up_weight), heads(down_weight)), z
    ).reshape(rows, -1)
    mixed_share = exchange(packed(heads(swish_weight), heads(output_weight)), z).reshape(rows, -1)
    feed_full = lax.all_gather(feed_share, "seq", axis_index_groups=planes, axis=0, tiled=True)
    qk_full = spread(retention_share[:, : 2 * DK], "x", "y", where)
    v_full = spread(retention_share[:, 2 * DK :], "y", "x", where)
    sw_full = spread(mixed_share[:, :DV], "x", "y", where)
    out_full = spread(mixed_share[:, DV:], "y", "x", where)
    gate_full, up_full, down_full = feed_full[:, :DV], feed_full[:, DV : 2 * DV], feed_full[:, 2 * DV :]

    tokens_own = own(tokens)
    tokens_all = gather_rows(tokens_own)
    upstream_own = own(cotangent)
    upstream_all = gather_rows(upstream_own)

    normal_one = layer_stats(tokens_all.astype(F32))[0]
    normed = (normal_one * mixer_gain + mixer_bias).astype(BF)

    number = jnp.arange(SIDE * rows)
    local_place = (
        ((z + number // half % SIDE) % SIDE) * rows
        + ((t + number // (SIDE * half)) % 2) * half
        + number % half
    )
    count = SIDE * rows
    positions = ((place // SIDE) * count + local_place).astype(F32)
    frequency = 1.0 / 10000.0 ** jnp.linspace(0.0, 1.0, DK // 2, dtype=F32)
    phases = positions[:, None] * frequency[None, :]
    cosine, sine = jnp.cos(phases), jnp.sin(phases)

    def turn(values):
        a, b = values[:, : DK // 2], values[:, DK // 2 :]
        return jnp.concatenate([a * cosine - b * sine, b * cosine + a * sine], axis=1)

    def turn_back(values):
        a, b = values[:, : DK // 2], values[:, DK // 2 :]
        return jnp.concatenate([a * cosine + b * sine, b * cosine - a * sine], axis=1)

    rate = jnp.log(1.0 - 2.0 ** (-5.0 - (SIDE * t + z).astype(F32)))
    places = local_place.astype(F32)
    offsets = places[:, None] - places[None, :]
    within = jnp.where(offsets >= 0, jnp.exp(jnp.maximum(offsets, 0.0) * rate), 0.0)
    onward = jnp.exp(places * rate)[:, None]
    leftover = jnp.exp((count - places) * rate)[:, None]
    carry = jnp.exp(count * rate)

    queries_keys = mm(normed, qk_full)
    query = turn(queries_keys[:, :DK]).astype(BF)
    key = (turn(queries_keys[:, DK:]) * DK ** (-0.5)).astype(BF)
    value = mm(normed, v_full).astype(BF)
    key_left = (key.astype(F32) * leftover).astype(BF)
    incoming = prefix(mm(key_left, value, 0, 0), carry, where, False).astype(BF)
    switch = mm(normed, sw_full)
    scores = (mm(query, key, 1, 1) * within).astype(BF)
    retained = mm(scores, value) + mm(query, incoming) * onward
    normal_ret, scale_ret = layer_stats(retained)
    swish_act = jax.nn.silu(switch)
    branch = (swish_act * normal_ret).astype(BF)
    attended = reduce_rows(mm(branch, out_full, 1, 1))

    residual_in = tokens_own.astype(F32)
    residual = residual_in + attended
    normal_two, scale_two = layer_stats(residual)
    normed_two = gather_rows((normal_two * feed_gain + feed_bias).astype(BF))
    gate_pre = mm(normed_two, gate_full)
    upward = mm(normed_two, up_full)
    gate_act = jax.nn.silu(gate_pre)
    inner_act = (gate_act * upward).astype(BF)
    grad_inner = mm(upstream_all, down_full)
    grad_gate = (grad_inner * upward * silu_slope(gate_pre)).astype(BF)
    grad_up = (grad_inner * gate_act).astype(BF)
    grad_norm_two = reduce_rows(mm(grad_gate, gate_full, 1, 1) + mm(grad_up, up_full, 1, 1))
    feed_out = reduce_rows(mm(inner_act, down_full, 1, 1))
    block_output = (residual + feed_out).astype(BF)
    upstream = upstream_own.astype(F32)
    grad_resid = upstream + norm_back(grad_norm_two * feed_gain, normal_two, scale_two)
    grad_attended = gather_rows(grad_resid.astype(BF))

    feed_terms = jnp.concatenate(
        [
            mm(normed_two, grad_gate, 0, 0).astype(BF),
            mm(normed_two, grad_up, 0, 0).astype(BF),
            mm(upstream_all, inner_act, 0, 0).astype(BF),
        ],
        axis=1,
    )
    feed_sum = lax.psum_scatter(
        feed_terms, "seq", axis_index_groups=planes, scatter_dimension=0, tiled=True
    )

    grad_branch = mm(grad_attended, out_full)
    grad_switch = (grad_branch * normal_ret * silu_slope(switch)).astype(BF)
    grad_low = norm_back(grad_branch * swish_act, normal_ret, scale_ret).astype(BF)
    grad_onward = (grad_low.astype(F32) * onward).astype(BF)
    outgoing = prefix(mm(query, grad_onward, 0, 0), carry, where, True).astype(BF)
    grad_scores = (mm(grad_low, value, 1, 1) * within).astype(BF)
    grad_query = mm(grad_scores, key) + mm(grad_onward, incoming, 1, 1)
    grad_key = mm(grad_scores, query, 0, 0) + mm(value, outgoing, 1, 1) * leftover
    grad_value = mm(scores, grad_low, 0, 0) + mm(key_left, outgoing)
    query_grads = turn_back(grad_query).astype(BF)
    key_grads = (turn_back(grad_key) * DK ** (-0.5)).astype(BF)
    qk_grads = jnp.concatenate([query_grads, key_grads], axis=1)
    value_grads = grad_value.astype(BF)
    share_one = (
        mm(qk_grads, qk_full, 1, 1)
        + mm(value_grads, v_full, 1, 1)
        + mm(grad_switch, sw_full, 1, 1)
    )
    grad_norm_one = reduce_rows(share_one)
    normal_own, scale_own = layer_stats(residual_in)
    tokens_grad = grad_resid + norm_back(grad_norm_one * mixer_gain, normal_own, scale_own)

    norm_terms = jnp.stack(
        [
            jnp.sum(share_one * normal_one, axis=0),
            jnp.sum(share_one, axis=0),
            jnp.sum(grad_norm_two * normal_two, axis=0),
            jnp.sum(grad_norm_two, axis=0),
        ]
    )
    coarse = norm_terms.astype(BF)
    fine = (norm_terms - coarse.astype(F32)).astype(BF)
    norm_columns = jnp.pad(jnp.concatenate([coarse, fine], axis=0).T, ((0, 0), (0, 120)))
    mixer_terms = jnp.concatenate(
        [
            mm(normed, qk_grads, 0, 0).astype(BF),
            mm(normed, value_grads, 0, 0).astype(BF),
            mm(normed, grad_switch, 0, 0).astype(BF),
            mm(grad_attended, branch, 0, 0).astype(BF),
            norm_columns,
        ],
        axis=1,
    )
    mixer_sum = lax.psum_scatter(
        mixer_terms, "seq", axis_index_groups=planes, scatter_dimension=0, tiled=True
    )

    feed_back = exchange(feed_sum.reshape(SIDE, shard, -1), z)
    mixer_back = exchange(mixer_sum.reshape(SIDE, shard, -1), z)

    def columns(blocks, start, size):
        return blocks[:, :, start : start + size].astype(F32).transpose(1, 0, 2).reshape(shard, -1)

    def join_pairs(blocks, start):
        part = blocks[:, :, start : start + DK].transpose(1, 0, 2).reshape(shard * SIDE, DK)
        return mm(part, shuffle, 1, 1).reshape(shard, SIDE * DK)

    norms = jnp.sum(mixer_back[:, :, 4 * DV :].astype(F32), axis=0)
    norms = norms + swap(norms)
    norms = (norms[:, :4] + norms[:, 4:8]).T

    def both_halves(values):
        theirs = swap(values)
        return jnp.concatenate(
            [jnp.where(t == 0, values, theirs), jnp.where(t == 0, theirs, values)], axis=0
        )

    return (
        both_halves(block_output),
        both_halves(tokens_grad),
        norms[0],
        norms[1],
        join_pairs(mixer_back, 0),
        join_pairs(mixer_back, DK),
        columns(mixer_back, DV, DV),
        columns(mixer_back, 2 * DV, DV),
        columns(mixer_back, 3 * DV, DV),
        norms[2],
        norms[3],
        columns(feed_back, 0, DV),
        columns(feed_back, DV, DV),
        columns(feed_back, 2 * DV, DV),
    )


def solution(mesh):
    split = P("seq", "tp")
    token = P("seq", None)
    in_specs = (token, P(), P()) + (split,) * 5 + (P(), P()) + (split,) * 3 + (token,)
    out_specs = (token, token, P("seq"), P("seq")) + (split,) * 5 + (P("seq"), P("seq")) + (split,) * 3
    return jax.shard_map(local, mesh=mesh, in_specs=in_specs, out_specs=out_specs, check_vma=False)
```

```python
import jax
import jax.numpy as jnp
from jax import lax
from jax.experimental import pallas as pl
from jax.experimental.pallas import tpu as pltpu
from jax.sharding import PartitionSpec as P

DK = 256
DV = 512
SIDE = 4
BF = jnp.bfloat16
F32 = jnp.float32
STRIDE = {"y": 16, "x": 4, "z": 1}


def pairs(axis, step):
    table = []
    for source in range(64):
        place = source // STRIDE[axis] % SIDE
        target = source + ((place - step) % SIDE - place) * STRIDE[axis]
        table.append((source, target))
    return table


def hop(value, axis, step):
    return lax.ppermute(value, "seq", pairs(axis, step % SIDE))


def swap(value):
    return lax.ppermute(value, "tp", [(0, 1), (1, 0)])


def direct(value, axis):
    return [value] + [hop(value, axis, step) for step in (1, 2, 3)]


def block(values, index, axis=0):
    return lax.dynamic_index_in_dim(values, index % SIDE, axis, keepdims=False)


def gather_rows(rows, beside=None):
    parts = direct(rows, "z")
    if beside is not None:
        parts[1], beside = lax.optimization_barrier((parts[1], beside))
    mine = jnp.concatenate(parts, axis=0)
    return (mine, swap(mine), beside)


def reduce_pair(own, other):
    return (own + swap(other.astype(BF)).astype(F32)).reshape(SIDE, -1, own.shape[-1])


def ring_shares(pair):
    return [pair[0]] + [hop(pair[step].astype(BF), "z", -step) for step in (1, 2, 3)]


def total_of(shares):
    return sum(share.astype(F32) for share in shares[1:]) + shares[0]


def whole(body, outs, scalars, *arrays, flops=0):
    vmem = pl.BlockSpec(memory_space=pltpu.VMEM)
    moved = sum(array.size * array.dtype.itemsize for array in [*arrays, *outs])
    if scalars.ndim == 0:
        scalars = scalars.reshape(1).astype(jnp.int32)
    return pl.pallas_call(
        body,
        out_shape=outs,
        in_specs=[pl.BlockSpec(memory_space=pltpu.SMEM)] + [vmem] * len(arrays),
        out_specs=[vmem] * len(outs),
        compiler_params=pltpu.CompilerParams(vmem_limit_bytes=40 * 2**20),
        cost_estimate=pl.CostEstimate(flops=flops, bytes_accessed=moved, transcendentals=0),
    )(scalars, *arrays)


def shaped(dtype, *shape):
    return jax.ShapeDtypeStruct(shape, dtype)


def head_of(z_ref, step):
    return lax.rem(z_ref[0] + SIDE + step, SIDE)


def lanes(ref, head, width):
    return ref[:, pl.ds(pl.multiple_of(head * width, width), width)]


def pack_body(z_ref, *refs):
    sources, pieces = refs[:8], refs[8 : 8 + 2 * SIDE]
    held, sems = refs[8 + 2 * SIDE : -1], refs[-1]
    copies = [
        pltpu.make_async_copy(source, ref, sems.at[place])
        for place, (source, ref) in enumerate(zip(sources, held))
    ]
    for copy in copies:
        copy.start()
    old = lax.broadcasted_iota(jnp.int32, (DK, DK), 0)
    new = lax.broadcasted_iota(jnp.int32, (DK, DK), 1)
    shuffle = (old == jnp.where(new < DK // 2, 2 * new, 2 * new - DK + 1)).astype(F32).astype(BF)
    for place, ref in enumerate(held):
        copies[place].wait()
        for step in range(SIDE):
            head = head_of(z_ref, -step)
            if place < 2:
                part = jnp.dot(lanes(ref, head, DK), shuffle, preferred_element_type=F32)
                pieces[step][:, place * DK : (place + 1) * DK] = part.astype(BF)
            elif place < 5:
                pieces[step][:, (place - 1) * DV : place * DV] = lanes(ref, head, DV)
            else:
                pieces[SIDE + step][:, (place - 5) * DV : (place - 4) * DV] = lanes(ref, head, DV)


def pack(z, weights):
    vmem = pl.BlockSpec(memory_space=pltpu.VMEM)
    shard = weights[0].shape[0]
    outs = [jax.ShapeDtypeStruct((shard, 2 * DK + 3 * DV), BF)] * SIDE
    outs = outs + [jax.ShapeDtypeStruct((shard, 3 * DV), BF)] * SIDE
    return pl.pallas_call(
        pack_body,
        out_shape=outs,
        in_specs=[pl.BlockSpec(memory_space=pltpu.SMEM)]
        + [pl.BlockSpec(memory_space=pl.ANY)] * len(weights),
        out_specs=[vmem] * len(outs),
        scratch_shapes=[pltpu.VMEM(weight.shape, BF) for weight in weights]
        + [pltpu.SemaphoreType.DMA((len(weights),))],
        compiler_params=pltpu.CompilerParams(vmem_limit_bytes=24 * 2**20),
    )(
        z.reshape(1).astype(jnp.int32),
        *[pltpu.with_memory_space_constraint(weight, pltpu.HBM) for weight in weights],
    )


def cut_body(z_ref, whole_ref, *pieces):
    height = pieces[0].shape[0]
    for step, piece in enumerate(pieces):
        row = pl.multiple_of(head_of(z_ref, -step) * height, height)
        piece[...] = whole_ref[pl.ds(row, height), :]


def unpack_body(paired, z_ref, *refs):
    outs = refs[SIDE:]
    old = lax.broadcasted_iota(jnp.int32, (DK, DK), 1)
    new = lax.broadcasted_iota(jnp.int32, (DK, DK), 0)
    shuffle = (old == jnp.where(new < DK // 2, 2 * new, 2 * new - DK + 1)).astype(F32).astype(BF)
    for step in range(SIDE):
        piece = refs[step]
        head = head_of(z_ref, step)
        start = 0
        for place, out in enumerate(outs):
            width = out.shape[1] // SIDE
            part = piece[:, start : start + width]
            if place in paired:
                part = jnp.dot(part, shuffle, preferred_element_type=F32)
            out[:, pl.ds(pl.multiple_of(head * width, width), width)] = part.astype(F32)
            start += width


def assemble_body(z_ref, *refs):
    for step in range(SIDE):
        piece = refs[step]
        height = piece.shape[0]
        row = pl.multiple_of(head_of(z_ref, step) * height, height)
        column = 0
        for whole_ref in refs[SIDE:]:
            width = whole_ref.shape[1]
            whole_ref[pl.ds(row, height), :] = piece[:, column : column + width]
            column += width


def grads_body(terms, turned, lefts, *refs):
    left, right, out = refs[:lefts], refs[lefts : lefts + terms[-1][-1][1] + 1], refs[-1]
    for place, term in enumerate(terms):

        @pl.when(pl.program_id(1) == place)
        def _(term=term):
            part = 0.0
            for a, b in term:
                part = part + mm(left[a][...], right[b][...], int(a in turned), 0)
            out[...] = part.astype(BF)


def grads(terms, lefts, turned, rights, blocks, first, into=None, rows=512):
    model = lefts[0].shape[0 if 0 in turned else 1]
    specs = [
        pl.BlockSpec((rows, left.shape[1]), lambda i, j: (i, 0))
        if place in turned
        else pl.BlockSpec((left.shape[0], rows), lambda i, j: (0, i))
        for place, left in enumerate(lefts)
    ]
    specs = specs + [pl.BlockSpec(right.shape, lambda i, j: (0, 0)) for right in rights]
    arrays = [*lefts, *rights]
    if into is not None:
        specs.append(pl.BlockSpec(memory_space=pl.ANY))
        arrays.append(into)
    width = len(terms) * DV
    return pl.pallas_call(
        lambda *refs: grads_body(terms, turned, len(lefts), *refs),
        grid=(model // rows, len(terms)),
        out_shape=pltpu.HBM((model, blocks * DV), BF),
        in_specs=specs,
        out_specs=pl.BlockSpec((rows, DV), lambda i, j: (i, first + j)),
        input_output_aliases={} if into is None else {len(arrays) - 1: 0},
        compiler_params=pltpu.CompilerParams(vmem_limit_bytes=32 * 2**20),
        cost_estimate=pl.CostEstimate(
            flops=2 * 512 * model * width, bytes_accessed=2 * model * (width + 512), transcendentals=0
        ),
    )(*arrays)


def norm_body(mine, theirs, gain, bias, out):
    def run(ref):
        values = ref[...].astype(F32)
        centred = values - jnp.mean(values, axis=-1, keepdims=True)
        scaling = lax.rsqrt(jnp.mean(centred * centred, axis=-1, keepdims=True) + 1e-05)
        out[...] = (centred * scaling * gain[...] + bias[...]).astype(BF)

    pl.when(pl.program_id(0) < SIDE)(lambda: run(mine))
    pl.when(pl.program_id(0) >= SIDE)(lambda: run(theirs))


def norm_rows(mine, theirs, gain, bias):
    size, model = mine.shape[0], gain.shape[0]
    part = size // SIDE
    vector = pl.BlockSpec((1, model), lambda i: (0, 0))
    return pl.pallas_call(
        norm_body,
        grid=(2 * SIDE,),
        out_shape=shaped(BF, 2 * size, model),
        in_specs=[
            pl.BlockSpec((part, model), lambda i: (jnp.minimum(i, SIDE - 1), 0)),
            pl.BlockSpec((part, model), lambda i: (jnp.maximum(i - SIDE, 0), 0)),
            vector,
            vector,
        ],
        out_specs=pl.BlockSpec((part, model), lambda i: (i, 0)),
        cost_estimate=pl.CostEstimate(
            flops=20 * size * model, bytes_accessed=12 * size * model, transcendentals=0
        ),
    )(mine, theirs, gain.reshape(1, -1), bias.reshape(1, -1))


def turn_body(rows, out):
    out[...] = rows[...].T


def turned(rows):
    size, model = rows.shape
    return pl.pallas_call(
        turn_body,
        grid=(model // size,),
        out_shape=shaped(rows.dtype, model, size),
        in_specs=[pl.BlockSpec((size, size), lambda i: (0, i))],
        out_specs=pl.BlockSpec((size, size), lambda i: (i, 0)),
        cost_estimate=pl.CostEstimate(
            flops=size * model, bytes_accessed=4 * size * model, transcendentals=0
        ),
    )(rows)


def state_body(x_ref, left, right, *pieces):
    for step, piece in enumerate(pieces):
        width = piece.shape[1]
        part = lax.dot_general(
            left[...],
            lanes(right, head_of(x_ref, -step), width),
            (((0,), (0,)), ((), ())),
            preferred_element_type=F32,
        )
        piece[...] = part.astype(piece.dtype)


def mix_body(weights, *refs):
    count = weights.shape[1]
    for place, out in enumerate(refs[count:]):
        total = 0.0
        for source in range(count):
            total = total + weights[place, source] * refs[source][...].astype(F32)
        out[...] = total.astype(out.dtype)


def quarters_body(x_ref, *refs):
    out = refs[-1]
    for step, piece in enumerate(refs[:-1]):
        width = piece.shape[1]
        start = pl.multiple_of(head_of(x_ref, step) * width, width)
        out[:, pl.ds(start, width)] = piece[...].astype(out.dtype)


def layer_stats(values):
    centred = values - jnp.mean(values, axis=-1, keepdims=True)
    scaling = lax.rsqrt(jnp.mean(centred * centred, axis=-1, keepdims=True) + 1e-05)
    return (centred * scaling, scaling)


def norm_back(grad_hat, normal, scaling):
    return scaling * (
        grad_hat
        - jnp.mean(grad_hat, axis=-1, keepdims=True)
        - normal * jnp.mean(grad_hat * normal, axis=-1, keepdims=True)
    )


def silu_slope(values):
    logistic = jax.nn.sigmoid(values)
    return logistic * (1.0 + values * (1.0 - logistic))


def mm(left, right, left_dim=1, right_dim=0):
    return lax.dot_general(
        left, right, (((left_dim,), (right_dim,)), ((), ())), preferred_element_type=F32
    )


def scan_weights(size, rate, where, backward):
    x, y = where["x"], where["y"]
    steps = jnp.arange(SIDE)

    def mirrored(index):
        return SIDE - 1 - index % SIDE if backward else index % SIDE

    def power(count):
        return jnp.exp(count.astype(F32) * size * rate)

    sources, targets = mirrored(x + steps), mirrored(x - steps)
    lines, line = mirrored(y + steps), mirrored(y)
    to_line = power(SIDE - 1 - sources)
    from_line = jnp.where(lines < line, power(SIDE * jnp.maximum(line - 1 - lines, 0)), 0.0)
    gap = targets[:, None] - 1 - sources[None, :]
    within = jnp.where(gap >= 0, power(jnp.maximum(gap, 0)), 0.0)
    reach = power(targets)[:, None] * from_line[None, 1:]
    return to_line[None, :], jnp.concatenate([within, reach], axis=1)


def scan(left, right, weights, where):
    x = where["x"]
    shape = (left.shape[1], right.shape[1] // SIDE)
    pieces = whole(state_body, [shaped(F32, *shape)] + [shaped(BF, *shape)] * 3, x, left, right)
    got = [pieces[0]] + [hop(pieces[step], "x", step) for step in (1, 2, 3)]
    (total,) = whole(mix_body, [shaped(BF, *shape)], weights[0], *got)
    others = [hop(total, "y", step) for step in (1, 2, 3)]
    given = whole(mix_body, [shaped(BF, *shape)] * SIDE, weights[1], *got, *others)
    moved = [given[0]] + [hop(given[step], "x", step) for step in (1, 2, 3)]
    (joined,) = whole(quarters_body, [shaped(BF, shape[0], right.shape[1])], x, *moved)
    return joined


def project_body(rows_in, weight_in, cosine, sine, left_over, query, key, value, key_left, rows, weight, sems):
    steps = weight.shape[0]
    copies = [pltpu.make_async_copy(rows_in, rows, sems.at[steps])]
    for step in range(steps):
        source = weight_in.at[:, pl.ds(step * DK, DK)]
        copies.append(pltpu.make_async_copy(source, weight.at[step], sems.at[step]))
    for copy in copies:
        copy.start()
    copies[0].wait()
    half = DK // 2
    for step in range(steps):
        copies[step + 1].wait()
        part = jnp.dot(rows[...], weight[step], preferred_element_type=F32)
        if step >= 2:
            value[:, (step - 2) * DK : (step - 1) * DK] = part.astype(BF)
            continue
        a, b = part[:, :half], part[:, half:]
        for place, whole_half in enumerate(
            (a * cosine[...] - b * sine[...], b * cosine[...] + a * sine[...])
        ):
            columns = slice(place * half, (place + 1) * half)
            if step == 0:
                query[:, columns] = whole_half.astype(BF)
            else:
                key[:, columns] = (whole_half * DK ** (-0.5)).astype(BF)
                key_left[:, columns] = (key[:, columns].astype(F32) * left_over[...]).astype(BF)


def project(rows, weight, cosine, sine, leftover):
    size, model = rows.shape
    vmem = pl.BlockSpec(memory_space=pltpu.VMEM)
    kept = pl.BlockSpec(memory_space=pl.ANY)
    steps = 2 + DV // DK
    return pl.pallas_call(
        project_body,
        out_shape=[
            shaped(BF, size, DK),
            shaped(BF, size, DK),
            shaped(BF, size, DV),
            shaped(BF, size, DK),
        ],
        in_specs=[kept, kept] + [vmem] * 3,
        out_specs=[vmem] * 4,
        scratch_shapes=[
            pltpu.VMEM((size, model), BF),
            pltpu.VMEM((steps, model, DK), BF),
            pltpu.SemaphoreType.DMA((steps + 1,)),
        ],
        compiler_params=pltpu.CompilerParams(vmem_limit_bytes=32 * 2**20),
        cost_estimate=pl.CostEstimate(
            flops=2 * size * model * steps * DK, bytes_accessed=2 * model * steps * DK, transcendentals=0
        ),
    )(
        pltpu.with_memory_space_constraint(rows, pltpu.HBM),
        pltpu.with_memory_space_constraint(weight, pltpu.HBM),
        cosine,
        sine,
        leftover,
    )


def feed_back_body(z_ref, first, second, weights, *outs):
    for rows, out in zip((first, second), outs):
        out[...] = jnp.dot(rows[...], weights[:, 2 * DV :], preferred_element_type=F32)


def feed_body(z_ref, mine, theirs, back_mine, back_theirs, weights, *outs):
    inner, grad_gate, grad_up = outs[:3]
    gate, up = weights[:, :DV], weights[:, DV : 2 * DV]
    size = mine.shape[0]
    halves = ((theirs, back_theirs, outs[4]), (mine, back_mine, outs[3]))
    for place, (rows, grad_inner, share) in enumerate(halves):
        gate_pre = jnp.dot(rows[...], gate, preferred_element_type=F32)
        upward = jnp.dot(rows[...], up, preferred_element_type=F32)
        logistic = jax.nn.sigmoid(gate_pre)
        gate_act = gate_pre * logistic
        slope = logistic * (1.0 + gate_pre * (1.0 - logistic))
        one = (grad_inner[...] * upward * slope).astype(BF)
        two = (grad_inner[...] * gate_act).astype(BF)
        kept = slice((1 - place) * size, (2 - place) * size)
        inner[kept, :] = (gate_act * upward).astype(BF)
        grad_gate[kept, :] = one
        grad_up[kept, :] = two
        share[...] = (mm(one, gate, 1, 1) + mm(two, up, 1, 1)).astype(share.dtype)


def feed_out_body(inner, weight, own, other):
    size = own.shape[0]
    own[...] = mm(inner[:size, :], weight[...], 1, 1)
    other[...] = mm(inner[size:, :], weight[...], 1, 1).astype(BF)


def feed_out_shares(inner, weights):
    size, model = inner.shape[0] // 2, weights.shape[0]
    return pl.pallas_call(
        feed_out_body,
        grid=(model // DV,),
        out_shape=[shaped(F32, size, model), shaped(BF, size, 2 * model)],
        in_specs=[
            pl.BlockSpec(inner.shape, lambda i: (0, 0)),
            pl.BlockSpec((DV, DV), lambda i: (i, 2)),
        ],
        out_specs=[
            pl.BlockSpec((size, DV), lambda i: (0, i)),
            pl.BlockSpec((size, DV), lambda i: (0, i + model // DV)),
        ],
        compiler_params=pltpu.CompilerParams(vmem_limit_bytes=24 * 2**20),
        cost_estimate=pl.CostEstimate(
            flops=4 * size * model * DV, bytes_accessed=10 * size * model, transcendentals=0
        ),
    )(inner, weights)


def last_share_body(qk, value, swish, qk_w, value_w, swish_w, kept, own, other):
    share = mm(qk[...], qk_w[...], 1, 1) + mm(value[...], value_w[...], 1, 1)
    share = share + mm(swish[...], swish_w[...], 1, 1)
    size = own.shape[0]
    own[...] = share[:size]
    other[...] = share[size:].astype(BF)


def last_share(rights, weights, joint):
    count, model = rights[0].shape[0], weights.shape[0]
    size = count // 2
    fixed = pl.BlockSpec((count, DV), lambda i: (0, 0))
    return pl.pallas_call(
        last_share_body,
        grid=(model // DV,),
        out_shape=[shaped(F32, size, model), shaped(BF, size, 2 * model)],
        in_specs=[fixed] * 3
        + [pl.BlockSpec((DV, DV), lambda i, j=j: (i, j)) for j in range(3)]
        + [pl.BlockSpec(memory_space=pl.ANY)],
        out_specs=[pl.BlockSpec((size, DV), lambda i: (0, i))] * 2,
        input_output_aliases={6: 1},
        compiler_params=pltpu.CompilerParams(vmem_limit_bytes=24 * 2**20),
        cost_estimate=pl.CostEstimate(
            flops=6 * count * model * DV, bytes_accessed=14 * count * model, transcendentals=0
        ),
    )(*rights, weights, weights, weights, joint)


def pair_body(z_ref, first, second, received, *outs):
    model = first.shape[1]
    height = outs[0].shape[0]
    for step, out in enumerate(outs):
        rows = slice(step * height, (step + 1) * height)
        for place, ref in enumerate((first, second)):
            columns = slice(place * model, (place + 1) * model)
            out[:, columns] = (ref[rows, :] + received[rows, columns].astype(F32)).astype(out.dtype)


def reduce_line(values, axis, dim, where):
    here = where[axis]
    total = block(values, here, dim)
    for step in (1, 2, 3):
        total = total + hop(block(values, here - step, dim), axis, step)
    return total


def local(
    tokens,
    mixer_gain,
    mixer_bias,
    query_weight,
    key_weight,
    value_weight,
    swish_weight,
    output_weight,
    feed_gain,
    feed_bias,
    gate_weight,
    up_weight,
    down_weight,
    cotangent,
):
    place = lax.axis_index("seq")
    where = {"y": place // 16, "x": place // 4 % 4, "z": place % 4}
    z, t = where["z"], lax.axis_index("tp")
    rows = tokens.shape[0]
    half = rows // 2
    shard = query_weight.shape[0]
    planes = [[16 * b + 4 * a + c for b in range(4) for a in range(4)] for c in range(4)]

    def own(values):
        return lax.dynamic_slice_in_dim(values, t * half, half, 0)

    pieces = pack(
        z,
        [
            query_weight,
            key_weight,
            value_weight,
            swish_weight,
            output_weight,
            gate_weight,
            up_weight,
            down_weight,
        ],
    )

    def gathered(parts):
        moved = [parts[0]] + [hop(parts[step], "z", step) for step in (1, 2, 3)]
        (share,) = whole(
            assemble_body, [jax.ShapeDtypeStruct((rows, parts[0].shape[1]), BF)], z, *moved
        )
        return share

    mixer_share = gathered(pieces[:SIDE])
    mixer_full = lax.all_gather(mixer_share, "seq", axis_index_groups=planes, axis=0, tiled=True)
    feed_share = gathered(pieces[SIDE:])
    tokens_own, upstream_own = own(tokens), own(cotangent)
    model = tokens.shape[1]
    both_mine, both_theirs, _ = gather_rows(jnp.concatenate([tokens_own, upstream_own], axis=1))
    upstream_mine, upstream_theirs = both_mine[:, model:], both_theirs[:, model:]
    normed = norm_rows(both_mine, both_theirs, mixer_gain, mixer_bias)
    normed_turned = turned(normed)

    number = jnp.arange(SIDE * rows)
    local_place = (
        ((z + number // half % SIDE) % SIDE) * rows
        + ((t + number // (SIDE * half)) % 2) * half
        + number % half
    )
    count = SIDE * rows
    positions = ((place // SIDE) * count + local_place).astype(F32)
    frequency = 1.0 / 10000.0 ** jnp.linspace(0.0, 1.0, DK // 2, dtype=F32)
    phases = positions[:, None] * frequency[None, :]
    cosine, sine = jnp.cos(phases), jnp.sin(phases)

    def turn(values):
        a, b = values[:, : DK // 2], values[:, DK // 2 :]
        return jnp.concatenate([a * cosine - b * sine, b * cosine + a * sine], axis=1)

    def turn_back(values):
        a, b = values[:, : DK // 2], values[:, DK // 2 :]
        return jnp.concatenate([a * cosine + b * sine, b * cosine - a * sine], axis=1)

    rate = jnp.log(1.0 - 2.0 ** (-5.0 - (SIDE * t + z).astype(F32)))
    places = local_place.astype(F32)
    offsets = places[:, None] - places[None, :]
    within = jnp.where(offsets >= 0, jnp.exp(jnp.maximum(offsets, 0.0) * rate), 0.0)
    onward = jnp.exp(places * rate)[:, None]
    leftover = jnp.exp((count - places) * rate)[:, None]

    weights = [scan_weights(count, rate, where, backward) for backward in (False, True)]
    early = (
        feed_share,
        normed,
        normed_turned,
        upstream_mine,
        upstream_theirs,
        cosine,
        sine,
        within,
        leftover,
        onward,
        weights,
    )
    (
        feed_share,
        normed,
        normed_turned,
        upstream_mine,
        upstream_theirs,
        cosine,
        sine,
        within,
        leftover,
        onward,
        weights,
    ) = lax.optimization_barrier(early)
    feed_full = lax.all_gather(feed_share, "seq", axis_index_groups=planes, axis=0, tiled=True)
    query, key, value, key_left = project(normed, mixer_full, cosine, sine, leftover)
    mixer_rest, value = lax.optimization_barrier((mixer_full, value))
    sw_full, out_full = lax.optimization_barrier(
        (mixer_rest[:, 2 * DV : 3 * DV], mixer_rest[:, 3 * DV :])
    )
    key_left = (key.astype(F32) * leftover).astype(BF)
    incoming = scan(key_left, value, weights[0], where)
    switch = mm(normed, sw_full)
    scores = (mm(query, key, 1, 1) * within).astype(BF)
    retained = mm(scores, value) + mm(query, incoming) * onward
    normal_ret, scale_ret = layer_stats(retained)
    swish_act = jax.nn.silu(switch)
    branch = (swish_act * normal_ret).astype(BF)
    part = branch.shape[0] // 2
    pair_one = reduce_pair(mm(branch[:part], out_full, 1, 1), mm(branch[part:], out_full, 1, 1))
    shares_one = ring_shares(pair_one)
    grad_inner = whole(
        feed_back_body,
        [shaped(F32, part, DV)] * 2,
        z,
        upstream_mine,
        upstream_theirs,
        feed_full,
        flops=4 * part * upstream_mine.shape[1] * DV,
    )
    attended = total_of(shares_one)

    residual_in = tokens_own.astype(F32)
    residual = residual_in + attended
    normal_two, scale_two = layer_stats(residual)
    *normed_two, grad_inner = gather_rows(
        (normal_two * feed_gain + feed_bias).astype(BF), grad_inner
    )
    inner_act, grad_gate, grad_up, *feed_shares = whole(
        feed_body,
        [shaped(BF, count, DV)] * 3 + [shaped(F32, part, model), shaped(BF, part, model)],
        z,
        *normed_two,
        *grad_inner,
        feed_full,
        flops=16 * part * model * DV,
    )
    shares_two = ring_shares(reduce_pair(*feed_shares))
    halves = (slice(0, part), slice(part, count))
    feed_terms = grads(
        [[(0, 0), (1, 1)], [(0, 2), (1, 3)], [(2, 4), (3, 5)]],
        [*normed_two, upstream_mine, upstream_theirs],
        [],
        [array[rows_half] for array in (grad_gate, grad_up, inner_act) for rows_half in halves],
        3,
        0,
    )
    shares_two[1], feed_terms = lax.optimization_barrier((shares_two[1], feed_terms))
    feed_sum = lax.psum_scatter(
        feed_terms, "seq", axis_index_groups=planes, scatter_dimension=0, tiled=True
    )
    grad_norm_two = total_of(shares_two)
    upstream = upstream_own.astype(F32)
    grad_resid = upstream + norm_back(grad_norm_two * feed_gain, normal_two, scale_two)
    *grad_attended, _ = gather_rows(grad_resid.astype(BF))

    grad_branch = jnp.concatenate([mm(rows_half, out_full) for rows_half in grad_attended], axis=0)
    grad_switch = (grad_branch * normal_ret * silu_slope(switch)).astype(BF)
    grad_low = norm_back(grad_branch * swish_act, normal_ret, scale_ret).astype(BF)
    grad_onward = (grad_low.astype(F32) * onward).astype(BF)
    early_terms = grads(
        [[(0, 0)], [(1, 1), (2, 2)]],
        [normed_turned, *grad_attended],
        [0],
        [grad_switch, branch[:part], branch[part:]],
        4,
        0,
    )
    outgoing = scan(query, grad_onward, weights[1], where)
    grad_scores = (mm(grad_low, value, 1, 1) * within).astype(BF)
    grad_query = mm(grad_scores, key) + mm(grad_onward, incoming, 1, 1)
    grad_key = mm(grad_scores, query, 0, 0) + mm(value, outgoing, 1, 1) * leftover
    grad_value = mm(scores, grad_low, 0, 0) + mm(key_left, outgoing)
    query_grads = turn_back(grad_query).astype(BF)
    key_grads = (turn_back(grad_key) * DK ** (-0.5)).astype(BF)
    qk_grads = jnp.concatenate([query_grads, key_grads], axis=1)
    value_grads = grad_value.astype(BF)

    mixer_terms = grads(
        [[(0, 0)], [(0, 1)]], [normed_turned], [0], [qk_grads, value_grads], 4, 2, early_terms
    )
    mixer_terms, feed_sum = lax.optimization_barrier((mixer_terms, feed_sum))
    mixer_sum = lax.psum_scatter(
        mixer_terms, "seq", axis_index_groups=planes, scatter_dimension=0, tiled=True
    )

    mixer_terms, qk_grads, value_grads, grad_switch, inner_act = lax.optimization_barrier(
        (mixer_terms, qk_grads, value_grads, grad_switch, inner_act)
    )
    feed_own, joint = feed_out_shares(inner_act, feed_full)
    share_own, joint = last_share([qk_grads, value_grads, grad_switch], mixer_full, joint)
    joint_pair = whole(
        pair_body,
        [shaped(F32, half, 2 * model)] + [shaped(BF, half, 2 * model)] * 3,
        z,
        share_own,
        feed_own,
        swap(joint),
    )
    joint_total = total_of(
        [joint_pair[0]] + [hop(joint_pair[step], "z", -step) for step in (1, 2, 3)]
    )
    grad_norm_one = joint_total[:, :model]
    block_output = (residual + joint_total[:, model:]).astype(BF)
    normal_own, scale_own = layer_stats(residual_in)
    tokens_grad = grad_resid + norm_back(grad_norm_one * mixer_gain, normal_own, scale_own)
    norms = jnp.stack(
        [
            jnp.sum(grad_norm_one * normal_own, axis=0),
            jnp.sum(grad_norm_one, axis=0),
            jnp.sum(grad_norm_two * normal_two, axis=0),
            jnp.sum(grad_norm_two, axis=0),
        ]
    )
    norms = norms.reshape(4, SIDE, SIDE, SIDE, -1).transpose(1, 2, 3, 0, 4)
    norms = norms.reshape(SIDE, SIDE, SIDE, -1)
    for axis, dim in (("x", 1), ("y", 0), ("z", 0)):
        norms = reduce_line(norms, axis, dim, where)
    norms = norms.reshape(1, -1)
    norms = (norms + swap(norms)).reshape(4, -1)

    def cut_rows(summed):
        return whole(cut_body, [shaped(BF, shard, summed.shape[1])] * SIDE, z, summed)

    def returned(parts, widths, paired):
        moved = [parts[0]] + [hop(parts[step], "z", step) for step in (1, 2, 3)]
        outs = [shaped(F32, shard, SIDE * width) for width in widths]
        return whole(lambda *refs: unpack_body(paired, *refs), outs, z, *moved)

    gate_sum, up_sum, down_sum = returned(cut_rows(feed_sum), [DV] * 3, ())
    swish_sum, output_sum, query_sum, key_sum, value_sum = returned(
        cut_rows(mixer_sum), [DV, DV, DK, DK, DV], (2, 3)
    )

    def both_halves(values):
        theirs = swap(values)
        return jnp.concatenate(
            [jnp.where(t == 0, values, theirs), jnp.where(t == 0, theirs, values)], axis=0
        )

    return (
        both_halves(block_output),
        both_halves(tokens_grad),
        norms[0],
        norms[1],
        query_sum,
        key_sum,
        value_sum,
        swish_sum,
        output_sum,
        norms[2],
        norms[3],
        gate_sum,
        up_sum,
        down_sum,
    )


def solution(mesh):
    split = P("seq", "tp")
    token = P("seq", None)
    in_specs = (token, P(), P()) + (split,) * 5 + (P(), P()) + (split,) * 3 + (token,)
    out_specs = (token, token, P("seq"), P("seq")) + (split,) * 5 + (P("seq"), P("seq")) + (split,) * 3
    return jax.shard_map(local, mesh=mesh, in_specs=in_specs, out_specs=out_specs, check_vma=False)
```

```python
import jax
import jax.numpy as jnp
from jax import lax
from jax.experimental import pallas as pl
from jax.experimental.pallas import tpu as pltpu
from jax.sharding import PartitionSpec as P

DK = 256
DV = 512
SIDE = 4
BF = jnp.bfloat16
F32 = jnp.float32
STRIDE = {"y": 16, "x": 4, "z": 1}


def pairs(axis, step):
    table = []
    for source in range(64):
        place = source // STRIDE[axis] % SIDE
        target = source + ((place - step) % SIDE - place) * STRIDE[axis]
        table.append((source, target))
    return table


def hop(value, axis, step):
    return lax.ppermute(value, "seq", pairs(axis, step % SIDE))


def swap(value):
    return lax.ppermute(value, "tp", [(0, 1), (1, 0)])


def direct(value, axis):
    return [value] + [hop(value, axis, step) for step in (1, 2, 3)]


def block(values, index, axis=0):
    return lax.dynamic_index_in_dim(values, index % SIDE, axis, keepdims=False)


def gather_rows(rows, beside=None):
    parts = direct(rows, "z")
    if beside is not None:
        parts[1], beside = lax.optimization_barrier((parts[1], beside))
    mine = jnp.concatenate(parts, axis=0)
    return (mine, swap(mine), beside)


def ring_shares(own, other, z, beside=None):
    received = swap(other.astype(BF))
    if beside is not None:
        received, beside = lax.optimization_barrier((received, beside))
    height, model = own.shape[0] // SIDE, own.shape[1]
    pair = whole(
        pair_body,
        [shaped(F32, height, model)] + [shaped(BF, height, model)] * 3,
        z,
        own,
        received,
    )
    return [pair[0]] + [hop(pair[step], "z", -step) for step in (1, 2, 3)], beside


def total_of(shares):
    return sum(share.astype(F32) for share in shares[1:]) + shares[0]


def whole(body, outs, scalars, *arrays, flops=0):
    vmem = pl.BlockSpec(memory_space=pltpu.VMEM)
    moved = sum(array.size * array.dtype.itemsize for array in [*arrays, *outs])
    if scalars.ndim == 0:
        scalars = scalars.reshape(1).astype(jnp.int32)
    return pl.pallas_call(
        body,
        out_shape=outs,
        in_specs=[pl.BlockSpec(memory_space=pltpu.SMEM)] + [vmem] * len(arrays),
        out_specs=[vmem] * len(outs),
        compiler_params=pltpu.CompilerParams(vmem_limit_bytes=16 * 2**20),
        cost_estimate=pl.CostEstimate(flops=flops, bytes_accessed=moved, transcendentals=0),
    )(scalars, *arrays)


def shaped(dtype, *shape):
    return jax.ShapeDtypeStruct(shape, dtype)


def head_of(z_ref, step):
    return lax.rem(z_ref[0] + SIDE + step, SIDE)


def lanes(ref, head, width):
    return ref[:, pl.ds(pl.multiple_of(head * width, width), width)]


def pack_body(z_ref, *refs):
    sources, pieces = refs[:8], refs[8 : 8 + 2 * SIDE]
    held, sems = refs[8 + 2 * SIDE : -1], refs[-1]
    copies = [
        pltpu.make_async_copy(source, ref, sems.at[place])
        for place, (source, ref) in enumerate(zip(sources, held))
    ]
    for copy in copies:
        copy.start()
    old = lax.broadcasted_iota(jnp.int32, (DK, DK), 0)
    new = lax.broadcasted_iota(jnp.int32, (DK, DK), 1)
    shuffle = (old == jnp.where(new < DK // 2, 2 * new, 2 * new - DK + 1)).astype(F32).astype(BF)
    for place, ref in enumerate(held):
        copies[place].wait()
        for step in range(SIDE):
            head = head_of(z_ref, -step)
            if place < 2:
                part = jnp.dot(lanes(ref, head, DK), shuffle, preferred_element_type=F32)
                pieces[step][:, place * DK : (place + 1) * DK] = part.astype(BF)
            elif place < 5:
                pieces[step][:, (place - 1) * DV : place * DV] = lanes(ref, head, DV)
            else:
                pieces[SIDE + step][:, (place - 5) * DV : (place - 4) * DV] = lanes(ref, head, DV)


def pack(z, weights):
    vmem = pl.BlockSpec(memory_space=pltpu.VMEM)
    shard = weights[0].shape[0]
    outs = [jax.ShapeDtypeStruct((shard, 2 * DK + 3 * DV), BF)] * SIDE
    outs = outs + [jax.ShapeDtypeStruct((shard, 3 * DV), BF)] * SIDE
    return pl.pallas_call(
        pack_body,
        out_shape=outs,
        in_specs=[pl.BlockSpec(memory_space=pltpu.SMEM)]
        + [pl.BlockSpec(memory_space=pl.ANY)] * len(weights),
        out_specs=[vmem] * len(outs),
        scratch_shapes=[pltpu.VMEM(weight.shape, BF) for weight in weights]
        + [pltpu.SemaphoreType.DMA((len(weights),))],
        compiler_params=pltpu.CompilerParams(vmem_limit_bytes=16 * 2**20),
    )(
        z.reshape(1).astype(jnp.int32),
        *[pltpu.with_memory_space_constraint(weight, pltpu.HBM) for weight in weights],
    )


def cut_body(z_ref, whole_ref, *pieces):
    height = pieces[0].shape[0]
    for step, piece in enumerate(pieces):
        row = pl.multiple_of(head_of(z_ref, -step) * height, height)
        piece[...] = whole_ref[pl.ds(row, height), :]


def unpack_body(paired, z_ref, *refs):
    outs = refs[SIDE:]
    old = lax.broadcasted_iota(jnp.int32, (DK, DK), 1)
    new = lax.broadcasted_iota(jnp.int32, (DK, DK), 0)
    shuffle = (old == jnp.where(new < DK // 2, 2 * new, 2 * new - DK + 1)).astype(F32).astype(BF)
    for step in range(SIDE):
        piece = refs[step]
        head = head_of(z_ref, step)
        start = 0
        for place, out in enumerate(outs):
            width = out.shape[1] // SIDE
            part = piece[:, start : start + width]
            if place in paired:
                part = jnp.dot(part, shuffle, preferred_element_type=F32)
            out[:, pl.ds(pl.multiple_of(head * width, width), width)] = part.astype(F32)
            start += width


def assemble_body(z_ref, *refs):
    for step in range(SIDE):
        piece = refs[step]
        height = piece.shape[0]
        row = pl.multiple_of(head_of(z_ref, step) * height, height)
        column = 0
        for whole_ref in refs[SIDE:]:
            width = whole_ref.shape[1]
            whole_ref[pl.ds(row, height), :] = piece[:, column : column + width]
            column += width


def grads_body(terms, turned, lefts, *refs):
    left, right, out = refs[:lefts], refs[lefts : lefts + terms[-1][-1][1] + 1], refs[-1]
    for place, term in enumerate(terms):
        part = 0.0
        for a, b in term:
            part = part + mm(left[a][...], right[b][...], int(a in turned), 0)
        out[:, place * DV : (place + 1) * DV] = part.astype(BF)


def grads(terms, lefts, turned, rights, groups=1, group=0, into=None, rows=512):
    model = lefts[0].shape[0 if 0 in turned else 1]
    specs = [
        pl.BlockSpec((rows, left.shape[1]), lambda i: (i, 0))
        if place in turned
        else pl.BlockSpec((left.shape[0], rows), lambda i: (0, i))
        for place, left in enumerate(lefts)
    ]
    specs = specs + [pl.BlockSpec(right.shape, lambda i: (0, 0)) for right in rights]
    arrays = [*lefts, *rights]
    if into is not None:
        specs.append(pl.BlockSpec(memory_space=pl.ANY))
        arrays.append(into)
    width = len(terms) * DV
    return pl.pallas_call(
        lambda *refs: grads_body(terms, turned, len(lefts), *refs),
        grid=(model // rows,),
        out_shape=pltpu.HBM((model, groups * width), BF),
        in_specs=specs,
        out_specs=pl.BlockSpec((rows, width), lambda i: (i, group)),
        input_output_aliases={} if into is None else {len(arrays) - 1: 0},
        compiler_params=pltpu.CompilerParams(vmem_limit_bytes=20 * 2**20),
        cost_estimate=pl.CostEstimate(
            flops=2 * 512 * model * width, bytes_accessed=2 * model * (width + 512), transcendentals=0
        ),
    )(*arrays)


def norm_body(mine, theirs, gain, bias, out):
    def run(ref):
        values = ref[...].astype(F32)
        centred = values - jnp.mean(values, axis=-1, keepdims=True)
        scaling = lax.rsqrt(jnp.mean(centred * centred, axis=-1, keepdims=True) + 1e-05)
        out[...] = (centred * scaling * gain[...] + bias[...]).astype(BF)

    pl.when(pl.program_id(0) < SIDE)(lambda: run(mine))
    pl.when(pl.program_id(0) >= SIDE)(lambda: run(theirs))


def norm_rows(mine, theirs, gain, bias):
    size, model = mine.shape[0], gain.shape[0]
    part = size // SIDE
    vector = pl.BlockSpec((1, model), lambda i: (0, 0))
    return pl.pallas_call(
        norm_body,
        grid=(2 * SIDE,),
        out_shape=shaped(BF, 2 * size, model),
        in_specs=[
            pl.BlockSpec((part, model), lambda i: (jnp.minimum(i, SIDE - 1), 0)),
            pl.BlockSpec((part, model), lambda i: (jnp.maximum(i - SIDE, 0), 0)),
            vector,
            vector,
        ],
        out_specs=pl.BlockSpec((part, model), lambda i: (i, 0)),
        cost_estimate=pl.CostEstimate(
            flops=20 * size * model, bytes_accessed=12 * size * model, transcendentals=0
        ),
    )(mine, theirs, gain.reshape(1, -1), bias.reshape(1, -1))


def turn_body(rows, out):
    out[...] = rows[...].T


def turned(rows):
    size, model = rows.shape
    return pl.pallas_call(
        turn_body,
        grid=(model // size,),
        out_shape=shaped(rows.dtype, model, size),
        in_specs=[pl.BlockSpec((size, size), lambda i: (0, i))],
        out_specs=pl.BlockSpec((size, size), lambda i: (i, 0)),
        cost_estimate=pl.CostEstimate(
            flops=size * model, bytes_accessed=4 * size * model, transcendentals=0
        ),
    )(rows)


def state_body(x_ref, left, right, *pieces):
    for step, piece in enumerate(pieces):
        width = piece.shape[1]
        part = lax.dot_general(
            left[...],
            lanes(right, head_of(x_ref, -step), width),
            (((0,), (0,)), ((), ())),
            preferred_element_type=F32,
        )
        piece[...] = part.astype(piece.dtype)


def mix_body(weights, *refs):
    count = weights.shape[1]
    for place, out in enumerate(refs[count:]):
        total = 0.0
        for source in range(count):
            total = total + weights[place, source] * refs[source][...].astype(F32)
        out[...] = total.astype(out.dtype)


def quarters_body(x_ref, *refs):
    out = refs[-1]
    for step, piece in enumerate(refs[:-1]):
        width = piece.shape[1]
        start = pl.multiple_of(head_of(x_ref, step) * width, width)
        out[:, pl.ds(start, width)] = piece[...].astype(out.dtype)


def layer_stats(values):
    centred = values - jnp.mean(values, axis=-1, keepdims=True)
    scaling = lax.rsqrt(jnp.mean(centred * centred, axis=-1, keepdims=True) + 1e-05)
    return (centred * scaling, scaling)


def norm_back(grad_hat, normal, scaling):
    return scaling * (
        grad_hat
        - jnp.mean(grad_hat, axis=-1, keepdims=True)
        - normal * jnp.mean(grad_hat * normal, axis=-1, keepdims=True)
    )


def silu_slope(values):
    logistic = jax.nn.sigmoid(values)
    return logistic * (1.0 + values * (1.0 - logistic))


def mm(left, right, left_dim=1, right_dim=0):
    return lax.dot_general(
        left, right, (((left_dim,), (right_dim,)), ((), ())), preferred_element_type=F32
    )


def scan_weights(size, rate, where, backward):
    x, y = where["x"], where["y"]
    steps = jnp.arange(SIDE)

    def mirrored(index):
        return SIDE - 1 - index % SIDE if backward else index % SIDE

    def power(count):
        return jnp.exp(count.astype(F32) * size * rate)

    sources, targets = mirrored(x + steps), mirrored(x - steps)
    lines, line = mirrored(y + steps), mirrored(y)
    to_line = power(SIDE - 1 - sources)
    from_line = jnp.where(lines < line, power(SIDE * jnp.maximum(line - 1 - lines, 0)), 0.0)
    gap = targets[:, None] - 1 - sources[None, :]
    within = jnp.where(gap >= 0, power(jnp.maximum(gap, 0)), 0.0)
    reach = power(targets)[:, None] * from_line[None, 1:]
    return to_line[None, :], jnp.concatenate([within, reach], axis=1)


def scan(left, right, weights, where, beside):
    x = where["x"]
    shape = (left.shape[1], right.shape[1] // SIDE)
    pieces = whole(state_body, [shaped(F32, *shape)] + [shaped(BF, *shape)] * 3, x, left, right)
    got = [pieces[0]] + [hop(pieces[step], "x", step) for step in (1, 2, 3)]
    (total,) = whole(mix_body, [shaped(BF, *shape)], weights[0], *got)
    others = [hop(total, "y", step) for step in (1, 2, 3)]
    given = whole(mix_body, [shaped(BF, *shape)] * SIDE, weights[1], *got, *others)
    moved = [given[0]] + [hop(given[step], "x", step) for step in (1, 2, 3)]
    if beside is not None:
        moved[1], beside = lax.optimization_barrier((moved[1], beside))
    (joined,) = whole(quarters_body, [shaped(BF, shape[0], right.shape[1])], x, *moved)
    return joined, beside


def project_body(rows_in, weight_in, cosine, sine, left_over, query, key, value, key_left, rows, weight, sems):
    width = weight.shape[1]
    depth = weight.shape[0] // SIDE
    copies = []
    for step in range(SIDE):
        part = pl.ds(step * depth, depth)
        source = weight_in.at[part, pl.ds(0, width)]
        copies.append(pltpu.make_async_copy(source, weight.at[part], sems.at[2 * step]))
        source = rows_in.at[:, part]
        copies.append(pltpu.make_async_copy(source, rows.at[:, part], sems.at[2 * step + 1]))
    for copy in copies:
        copy.start()
    total = 0.0
    for step in range(SIDE):
        copies[2 * step].wait()
        copies[2 * step + 1].wait()
        part = slice(step * depth, (step + 1) * depth)
        total = total + jnp.dot(rows[:, part], weight[part, :], preferred_element_type=F32)
    half = DK // 2
    for place in range(2):
        a = total[:, place * DK : place * DK + half]
        b = total[:, place * DK + half : (place + 1) * DK]
        turned_halves = (a * cosine[...] - b * sine[...], b * cosine[...] + a * sine[...])
        for index, turned_half in enumerate(turned_halves):
            columns = slice(index * half, (index + 1) * half)
            if place == 0:
                query[:, columns] = turned_half.astype(BF)
            else:
                key[:, columns] = (turned_half * DK ** (-0.5)).astype(BF)
                key_left[:, columns] = (key[:, columns].astype(F32) * left_over[...]).astype(BF)
    value[...] = total[:, 2 * DK :].astype(BF)


def project(rows, weight, cosine, sine, leftover):
    size, model = rows.shape
    vmem = pl.BlockSpec(memory_space=pltpu.VMEM)
    kept = pl.BlockSpec(memory_space=pl.ANY)
    steps = 2 + DV // DK
    return pl.pallas_call(
        project_body,
        out_shape=[
            shaped(BF, size, DK),
            shaped(BF, size, DK),
            shaped(BF, size, DV),
            shaped(BF, size, DK),
        ],
        in_specs=[kept, kept] + [vmem] * 3,
        out_specs=[vmem] * 4,
        scratch_shapes=[
            pltpu.VMEM((size, model), BF),
            pltpu.VMEM((model, steps * DK), BF),
            pltpu.SemaphoreType.DMA((2 * SIDE,)),
        ],
        compiler_params=pltpu.CompilerParams(vmem_limit_bytes=20 * 2**20),
        cost_estimate=pl.CostEstimate(
            flops=2 * size * model * steps * DK, bytes_accessed=2 * model * steps * DK, transcendentals=0
        ),
    )(
        pltpu.with_memory_space_constraint(rows, pltpu.HBM),
        pltpu.with_memory_space_constraint(weight, pltpu.HBM),
        cosine,
        sine,
        leftover,
    )


def feed_back_body(z_ref, first, second, weights, *outs):
    for rows, out in zip((first, second), outs):
        out[...] = jnp.dot(rows[...], weights[:, 2 * DV :], preferred_element_type=F32)


def feed_body(z_ref, mine, theirs, back_mine, back_theirs, weights, *outs):
    inner, grad_gate, grad_up = outs[:3]
    gate, up = weights[:, :DV], weights[:, DV : 2 * DV]
    size = mine.shape[0]
    halves = ((theirs, back_theirs, outs[4]), (mine, back_mine, outs[3]))
    for place, (rows, grad_inner, share) in enumerate(halves):
        gate_pre = jnp.dot(rows[...], gate, preferred_element_type=F32)
        upward = jnp.dot(rows[...], up, preferred_element_type=F32)
        logistic = jax.nn.sigmoid(gate_pre)
        gate_act = gate_pre * logistic
        slope = logistic * (1.0 + gate_pre * (1.0 - logistic))
        one = (grad_inner[...] * upward * slope).astype(BF)
        two = (grad_inner[...] * gate_act).astype(BF)
        kept = slice((1 - place) * size, (2 - place) * size)
        inner[kept, :] = (gate_act * upward).astype(BF)
        grad_gate[kept, :] = one
        grad_up[kept, :] = two
        share[...] = (mm(one, gate, 1, 1) + mm(two, up, 1, 1)).astype(share.dtype)


def feed_out_body(inner, weight, own, other):
    size = own.shape[0]
    own[...] = mm(inner[:size, :], weight[...], 1, 1)
    other[...] = mm(inner[size:, :], weight[...], 1, 1).astype(BF)


def feed_out_shares(inner, weights):
    size, model = inner.shape[0] // 2, weights.shape[0]
    return pl.pallas_call(
        feed_out_body,
        grid=(model // DV,),
        out_shape=[shaped(F32, size, model), shaped(BF, size, 2 * model)],
        in_specs=[
            pl.BlockSpec(inner.shape, lambda i: (0, 0)),
            pl.BlockSpec((DV, DV), lambda i: (i, 2)),
        ],
        out_specs=[
            pl.BlockSpec((size, DV), lambda i: (0, i)),
            pl.BlockSpec((size, DV), lambda i: (0, i + model // DV)),
        ],
        compiler_params=pltpu.CompilerParams(vmem_limit_bytes=16 * 2**20),
        cost_estimate=pl.CostEstimate(
            flops=4 * size * model * DV, bytes_accessed=10 * size * model, transcendentals=0
        ),
    )(inner, pltpu.with_memory_space_constraint(weights, pltpu.HBM))


def last_share_body(qk, value, swish, qk_w, value_w, swish_w, kept, own, other):
    share = mm(qk[...], qk_w[...], 1, 1) + mm(value[...], value_w[...], 1, 1)
    share = share + mm(swish[...], swish_w[...], 1, 1)
    size = own.shape[0]
    own[...] = share[:size]
    other[...] = share[size:].astype(BF)


def last_share(rights, weights, joint):
    count, model = rights[0].shape[0], weights.shape[0]
    size = count // 2
    fixed = pl.BlockSpec((count, DV), lambda i: (0, 0))
    return pl.pallas_call(
        last_share_body,
        grid=(model // DV,),
        out_shape=[shaped(F32, size, model), shaped(BF, size, 2 * model)],
        in_specs=[fixed] * 3
        + [pl.BlockSpec((DV, DV), lambda i, j=j: (i, j)) for j in range(3)]
        + [pl.BlockSpec(memory_space=pl.ANY)],
        out_specs=[pl.BlockSpec((size, DV), lambda i: (0, i))] * 2,
        input_output_aliases={6: 1},
        compiler_params=pltpu.CompilerParams(vmem_limit_bytes=16 * 2**20),
        cost_estimate=pl.CostEstimate(
            flops=6 * count * model * DV, bytes_accessed=14 * count * model, transcendentals=0
        ),
    )(*rights, *[pltpu.with_memory_space_constraint(weights, pltpu.HBM)] * 3, joint)


def pair_body(z_ref, *refs):
    owns, received, outs = refs[: -SIDE - 1], refs[-SIDE - 1], refs[-SIDE:]
    height = outs[0].shape[0]
    for step, out in enumerate(outs):
        rows = slice(step * height, (step + 1) * height)
        column = 0
        for ref in owns:
            columns = slice(column, column + ref.shape[1])
            out[:, columns] = (ref[rows, :] + received[rows, columns].astype(F32)).astype(out.dtype)
            column += ref.shape[1]


def reduce_line(values, axis, dim, where):
    here = where[axis]
    total = block(values, here, dim)
    for step in (1, 2, 3):
        total = total + hop(block(values, here - step, dim), axis, step)
    return total


def local(
    tokens,
    mixer_gain,
    mixer_bias,
    query_weight,
    key_weight,
    value_weight,
    swish_weight,
    output_weight,
    feed_gain,
    feed_bias,
    gate_weight,
    up_weight,
    down_weight,
    cotangent,
):
    place = lax.axis_index("seq")
    where = {"y": place // 16, "x": place // 4 % 4, "z": place % 4}
    z, t = where["z"], lax.axis_index("tp")
    rows = tokens.shape[0]
    half = rows // 2
    shard = query_weight.shape[0]
    planes = [[16 * b + 4 * a + c for b in range(4) for a in range(4)] for c in range(4)]

    def own(values):
        return lax.dynamic_slice_in_dim(values, t * half, half, 0)

    pieces = pack(
        z,
        [
            query_weight,
            key_weight,
            value_weight,
            swish_weight,
            output_weight,
            gate_weight,
            up_weight,
            down_weight,
        ],
    )

    def gathered(parts):
        moved = [parts[0]] + [hop(parts[step], "z", step) for step in (1, 2, 3)]
        (share,) = whole(
            assemble_body, [jax.ShapeDtypeStruct((rows, parts[0].shape[1]), BF)], z, *moved
        )
        return share

    mixer_share = gathered(pieces[:SIDE])
    mixer_full = lax.all_gather(mixer_share, "seq", axis_index_groups=planes, axis=0, tiled=True)
    feed_share = gathered(pieces[SIDE:])
    tokens_own, upstream_own = own(tokens), own(cotangent)
    model = tokens.shape[1]
    both_mine, both_theirs, _ = gather_rows(jnp.concatenate([tokens_own, upstream_own], axis=1))
    upstream_mine, upstream_theirs = both_mine[:, model:], both_theirs[:, model:]
    normed = norm_rows(both_mine, both_theirs, mixer_gain, mixer_bias)
    normed_turned = turned(normed)

    number = jnp.arange(SIDE * rows)
    local_place = (
        ((z + number // half % SIDE) % SIDE) * rows
        + ((t + number // (SIDE * half)) % 2) * half
        + number % half
    )
    count = SIDE * rows
    positions = ((place // SIDE) * count + local_place).astype(F32)
    frequency = 1.0 / 10000.0 ** jnp.linspace(0.0, 1.0, DK // 2, dtype=F32)
    phases = positions[:, None] * frequency[None, :]
    cosine, sine = jnp.cos(phases), jnp.sin(phases)

    def turn(values):
        a, b = values[:, : DK // 2], values[:, DK // 2 :]
        return jnp.concatenate([a * cosine - b * sine, b * cosine + a * sine], axis=1)

    def turn_back(values):
        a, b = values[:, : DK // 2], values[:, DK // 2 :]
        return jnp.concatenate([a * cosine + b * sine, b * cosine - a * sine], axis=1)

    rate = jnp.log(1.0 - 2.0 ** (-5.0 - (SIDE * t + z).astype(F32)))
    places = local_place.astype(F32)
    offsets = places[:, None] - places[None, :]
    within = jnp.where(offsets >= 0, jnp.exp(jnp.maximum(offsets, 0.0) * rate), 0.0)
    onward = jnp.exp(places * rate)[:, None]
    leftover = jnp.exp((count - places) * rate)[:, None]

    weights = [scan_weights(count, rate, where, backward) for backward in (False, True)]
    early = (
        feed_share,
        normed,
        normed_turned,
        upstream_mine,
        upstream_theirs,
        cosine,
        sine,
        within,
        leftover,
        onward,
        weights,
    )
    (
        feed_share,
        normed,
        normed_turned,
        upstream_mine,
        upstream_theirs,
        cosine,
        sine,
        within,
        leftover,
        onward,
        weights,
    ) = lax.optimization_barrier(early)
    feed_full = lax.all_gather(feed_share, "seq", axis_index_groups=planes, axis=0, tiled=True)
    query, key, value, key_left = project(normed, mixer_full, cosine, sine, leftover)
    mixer_rest, value = lax.optimization_barrier((mixer_full, value))
    sw_full, out_full = lax.optimization_barrier(
        (mixer_rest[:, 2 * DV : 3 * DV], mixer_rest[:, 3 * DV :])
    )
    key_left = (key.astype(F32) * leftover).astype(BF)
    incoming, switch = scan(key_left, value, weights[0], where, mm(normed, sw_full))
    scores = (mm(query, key, 1, 1) * within).astype(BF)
    retained = mm(scores, value) + mm(query, incoming) * onward
    normal_ret, scale_ret = layer_stats(retained)
    swish_act = jax.nn.silu(switch)
    branch = (swish_act * normal_ret).astype(BF)
    part = branch.shape[0] // 2
    shares_one, _ = ring_shares(
        mm(branch[:part], out_full, 1, 1), mm(branch[part:], out_full, 1, 1), z
    )
    grad_inner = whole(
        feed_back_body,
        [shaped(F32, part, DV)] * 2,
        z,
        upstream_mine,
        upstream_theirs,
        feed_full,
        flops=4 * part * upstream_mine.shape[1] * DV,
    )
    attended = total_of(shares_one)

    residual_in = tokens_own.astype(F32)
    residual = residual_in + attended
    normal_two, scale_two = layer_stats(residual)
    *normed_two, grad_inner = gather_rows(
        (normal_two * feed_gain + feed_bias).astype(BF), grad_inner
    )
    inner_act, grad_gate, grad_up, *feed_shares = whole(
        feed_body,
        [shaped(BF, count, DV)] * 3 + [shaped(F32, part, model), shaped(BF, part, model)],
        z,
        *normed_two,
        *grad_inner,
        feed_full,
        flops=16 * part * model * DV,
    )
    halves = (slice(0, part), slice(part, count))
    feed_terms = grads(
        [[(0, 0), (1, 1)], [(0, 2), (1, 3)], [(2, 4), (3, 5)]],
        [*normed_two, upstream_mine, upstream_theirs],
        [],
        [array[rows_half] for array in (grad_gate, grad_up, inner_act) for rows_half in halves],
    )
    shares_two, feed_terms = ring_shares(*feed_shares, z, feed_terms)
    feed_sum = lax.psum_scatter(
        feed_terms, "seq", axis_index_groups=planes, scatter_dimension=0, tiled=True
    )
    grad_norm_two = total_of(shares_two)
    upstream = upstream_own.astype(F32)
    grad_resid = upstream + norm_back(grad_norm_two * feed_gain, normal_two, scale_two)
    *grad_attended, _ = gather_rows(grad_resid.astype(BF))

    grad_branch = jnp.concatenate([mm(rows_half, out_full) for rows_half in grad_attended], axis=0)
    grad_switch = (grad_branch * normal_ret * silu_slope(switch)).astype(BF)
    grad_low = norm_back(grad_branch * swish_act, normal_ret, scale_ret).astype(BF)
    grad_onward = (grad_low.astype(F32) * onward).astype(BF)
    early_terms = grads(
        [[(0, 0)], [(1, 1), (2, 2)]],
        [normed_turned, *grad_attended],
        [0],
        [grad_switch, branch[:part], branch[part:]],
        2,
        0,
    )
    outgoing, _ = scan(query, grad_onward, weights[1], where, None)
    grad_scores = (mm(grad_low, value, 1, 1) * within).astype(BF)
    grad_query = mm(grad_scores, key) + mm(grad_onward, incoming, 1, 1)
    grad_key = mm(grad_scores, query, 0, 0) + mm(value, outgoing, 1, 1) * leftover
    grad_value = mm(scores, grad_low, 0, 0) + mm(key_left, outgoing)
    query_grads = turn_back(grad_query).astype(BF)
    key_grads = (turn_back(grad_key) * DK ** (-0.5)).astype(BF)
    qk_grads = jnp.concatenate([query_grads, key_grads], axis=1)
    value_grads = grad_value.astype(BF)

    mixer_terms = grads(
        [[(0, 0)], [(0, 1)]], [normed_turned], [0], [qk_grads, value_grads], 2, 1, early_terms
    )
    mixer_terms, feed_sum = lax.optimization_barrier((mixer_terms, feed_sum))
    mixer_sum = lax.psum_scatter(
        mixer_terms, "seq", axis_index_groups=planes, scatter_dimension=0, tiled=True
    )

    mixer_terms, qk_grads, value_grads, grad_switch, inner_act = lax.optimization_barrier(
        (mixer_terms, qk_grads, value_grads, grad_switch, inner_act)
    )
    feed_own, joint = feed_out_shares(inner_act, feed_full)
    share_own, joint = last_share([qk_grads, value_grads, grad_switch], mixer_full, joint)
    joint_pair = whole(
        pair_body,
        [shaped(F32, half, 2 * model)] + [shaped(BF, half, 2 * model)] * 3,
        z,
        share_own,
        feed_own,
        swap(joint),
    )
    joint_total = total_of(
        [joint_pair[0]] + [hop(joint_pair[step], "z", -step) for step in (1, 2, 3)]
    )
    grad_norm_one = joint_total[:, :model]
    block_output = (residual + joint_total[:, model:]).astype(BF)
    normal_own, scale_own = layer_stats(residual_in)
    tokens_grad = grad_resid + norm_back(grad_norm_one * mixer_gain, normal_own, scale_own)
    norms = jnp.stack(
        [
            jnp.sum(grad_norm_one * normal_own, axis=0),
            jnp.sum(grad_norm_one, axis=0),
            jnp.sum(grad_norm_two * normal_two, axis=0),
            jnp.sum(grad_norm_two, axis=0),
        ]
    )
    norms = norms.reshape(4, SIDE, SIDE, SIDE, -1).transpose(1, 2, 3, 0, 4)
    norms = norms.reshape(SIDE, SIDE, SIDE, -1)
    for axis, dim in (("x", 1), ("y", 0), ("z", 0)):
        norms = reduce_line(norms, axis, dim, where)
    norms = norms.reshape(1, -1)
    norms = (norms + swap(norms)).reshape(4, -1)

    def cut_rows(summed):
        return whole(cut_body, [shaped(BF, shard, summed.shape[1])] * SIDE, z, summed)

    def returned(parts, widths, paired):
        moved = [parts[0]] + [hop(parts[step], "z", step) for step in (1, 2, 3)]
        outs = [shaped(F32, shard, SIDE * width) for width in widths]
        return whole(lambda *refs: unpack_body(paired, *refs), outs, z, *moved)

    gate_sum, up_sum, down_sum = returned(cut_rows(feed_sum), [DV] * 3, ())
    swish_sum, output_sum, query_sum, key_sum, value_sum = returned(
        cut_rows(mixer_sum), [DV, DV, DK, DK, DV], (2, 3)
    )

    def both_halves(values):
        theirs = swap(values)
        return jnp.concatenate(
            [jnp.where(t == 0, values, theirs), jnp.where(t == 0, theirs, values)], axis=0
        )

    return (
        both_halves(block_output),
        both_halves(tokens_grad),
        norms[0],
        norms[1],
        query_sum,
        key_sum,
        value_sum,
        swish_sum,
        output_sum,
        norms[2],
        norms[3],
        gate_sum,
        up_sum,
        down_sum,
    )


def solution(mesh):
    split = P("seq", "tp")
    token = P("seq", None)
    in_specs = (token, P(), P()) + (split,) * 5 + (P(), P()) + (split,) * 3 + (token,)
    out_specs = (token, token, P("seq"), P("seq")) + (split,) * 5 + (P("seq"), P("seq")) + (split,) * 3
    return jax.shard_map(local, mesh=mesh, in_specs=in_specs, out_specs=out_specs, check_vma=False)
```

```python
import jax
import jax.numpy as jnp
from jax import lax
from jax.experimental import pallas as pl
from jax.experimental.pallas import tpu as pltpu
from jax.sharding import PartitionSpec as P

DK = 256
DV = 512
SIDE = 4
BF = jnp.bfloat16
F32 = jnp.float32
STRIDE = {"y": 16, "x": 4, "z": 1}


def pairs(axis, step):
    table = []
    for source in range(64):
        place = source // STRIDE[axis] % SIDE
        target = source + ((place - step) % SIDE - place) * STRIDE[axis]
        table.append((source, target))
    return table


def hop(value, axis, step):
    return lax.ppermute(value, "seq", pairs(axis, step % SIDE))


def swap(value):
    return lax.ppermute(value, "tp", [(0, 1), (1, 0)])


def direct(value, axis):
    return [value] + [hop(value, axis, step) for step in (1, 2, 3)]


def block(values, index, axis=0):
    return lax.dynamic_index_in_dim(values, index % SIDE, axis, keepdims=False)


def gather_rows(rows, beside=None):
    parts = direct(rows, "z")
    if beside is not None:
        parts[1], beside = lax.optimization_barrier((parts[1], beside))
    mine = jnp.concatenate(parts, axis=0)
    return (mine, swap(mine), beside)


def ring_shares(own, other, z):
    height, model = own.shape[0] // SIDE, own.shape[1]
    pair = whole(
        pair_body,
        [shaped(F32, height, model)] + [shaped(BF, height, model)] * 3,
        z,
        own,
        swap(other.astype(BF)),
    )
    return [pair[0]] + [hop(pair[step], "z", -step) for step in (1, 2, 3)]


def total_of(shares):
    return sum(share.astype(F32) for share in shares[1:]) + shares[0]


def whole(body, outs, scalars, *arrays, flops=0):
    vmem = pl.BlockSpec(memory_space=pltpu.VMEM)
    moved = sum(array.size * array.dtype.itemsize for array in arrays)
    if scalars.ndim == 0:
        scalars = scalars.reshape(1).astype(jnp.int32)
    return pl.pallas_call(
        body,
        out_shape=outs,
        in_specs=[pl.BlockSpec(memory_space=pltpu.SMEM)] + [vmem] * len(arrays),
        out_specs=[vmem] * len(outs),
        compiler_params=pltpu.CompilerParams(vmem_limit_bytes=16 * 2**20),
        cost_estimate=pl.CostEstimate(flops=flops, bytes_accessed=moved, transcendentals=0),
    )(scalars, *arrays)


def near(dtype, *shape):
    return pltpu.VMEM(shape, dtype)


def shaped(dtype, *shape):
    return jax.ShapeDtypeStruct(shape, dtype)


def head_of(z_ref, step):
    return lax.rem(z_ref[0] + SIDE + step, SIDE)


def lanes(ref, head, width):
    return ref[:, pl.ds(pl.multiple_of(head * width, width), width)]


def pack_body(z_ref, *refs):
    sources, pieces = refs[:8], refs[8 : 8 + 2 * SIDE]
    held, sems = refs[8 + 2 * SIDE : -1], refs[-1]
    copies = [
        pltpu.make_async_copy(source, ref, sems.at[place])
        for place, (source, ref) in enumerate(zip(sources, held))
    ]
    for copy in copies:
        copy.start()
    old = lax.broadcasted_iota(jnp.int32, (DK, DK), 0)
    new = lax.broadcasted_iota(jnp.int32, (DK, DK), 1)
    shuffle = (old == jnp.where(new < DK // 2, 2 * new, 2 * new - DK + 1)).astype(F32).astype(BF)
    for place, ref in enumerate(held):
        copies[place].wait()
        for step in range(SIDE):
            head = head_of(z_ref, -step)
            if place < 2:
                part = jnp.dot(lanes(ref, head, DK), shuffle, preferred_element_type=F32)
                pieces[step][:, place * DK : (place + 1) * DK] = part.astype(BF)
            elif place < 5:
                pieces[step][:, (place - 1) * DV : place * DV] = lanes(ref, head, DV)
            else:
                pieces[SIDE + step][:, (place - 5) * DV : (place - 4) * DV] = lanes(ref, head, DV)


def pack(z, weights):
    vmem = pl.BlockSpec(memory_space=pltpu.VMEM)
    shard = weights[0].shape[0]
    outs = [jax.ShapeDtypeStruct((shard, 2 * DK + 3 * DV), BF)] * SIDE
    outs = outs + [jax.ShapeDtypeStruct((shard, 3 * DV), BF)] * SIDE
    return pl.pallas_call(
        pack_body,
        out_shape=outs,
        in_specs=[pl.BlockSpec(memory_space=pltpu.SMEM)]
        + [pl.BlockSpec(memory_space=pl.ANY)] * len(weights),
        out_specs=[vmem] * len(outs),
        scratch_shapes=[pltpu.VMEM(weight.shape, BF) for weight in weights]
        + [pltpu.SemaphoreType.DMA((len(weights),))],
        compiler_params=pltpu.CompilerParams(vmem_limit_bytes=16 * 2**20),
    )(
        z.reshape(1).astype(jnp.int32),
        *[pltpu.with_memory_space_constraint(weight, pltpu.HBM) for weight in weights],
    )


def cut_body(z_ref, whole_ref, *pieces):
    height = pieces[0].shape[0]
    for step, piece in enumerate(pieces):
        row = pl.multiple_of(head_of(z_ref, -step) * height, height)
        piece[...] = whole_ref[pl.ds(row, height), :]


def unpack_body(paired, z_ref, *refs):
    outs = refs[SIDE:]
    old = lax.broadcasted_iota(jnp.int32, (DK, DK), 1)
    new = lax.broadcasted_iota(jnp.int32, (DK, DK), 0)
    shuffle = (old == jnp.where(new < DK // 2, 2 * new, 2 * new - DK + 1)).astype(F32).astype(BF)
    for step in range(SIDE):
        piece = refs[step]
        head = head_of(z_ref, step)
        start = 0
        for place, out in enumerate(outs):
            width = out.shape[1] // SIDE
            part = piece[:, start : start + width]
            if place in paired:
                part = jnp.dot(part, shuffle, preferred_element_type=F32)
            out[:, pl.ds(pl.multiple_of(head * width, width), width)] = part.astype(F32)
            start += width


def assemble_body(z_ref, *refs):
    for step in range(SIDE):
        piece = refs[step]
        height = piece.shape[0]
        row = pl.multiple_of(head_of(z_ref, step) * height, height)
        column = 0
        for whole_ref in refs[SIDE:]:
            width = whole_ref.shape[1]
            whole_ref[pl.ds(row, height), :] = piece[:, column : column + width]
            column += width


def grads_body(terms, turned, lefts, *refs):
    left, right, out = refs[:lefts], refs[lefts : lefts + terms[-1][-1][1] + 1], refs[-1]
    for place, term in enumerate(terms):
        part = 0.0
        for a, b in term:
            part = part + mm(left[a][...], right[b][...], int(a in turned), 0)
        out[:, place * DV : (place + 1) * DV] = part.astype(BF)


def grads(terms, lefts, turned, rights, groups=1, group=0, into=None, rows=512):
    model = lefts[0].shape[0 if 0 in turned else 1]
    specs = [
        pl.BlockSpec((rows, left.shape[1]), lambda i: (i, 0))
        if place in turned
        else pl.BlockSpec((left.shape[0], rows), lambda i: (0, i))
        for place, left in enumerate(lefts)
    ]
    specs = specs + [pl.BlockSpec(right.shape, lambda i: (0, 0)) for right in rights]
    arrays = [*lefts, *rights]
    if into is not None:
        specs.append(pl.BlockSpec(memory_space=pl.ANY))
        arrays.append(into)
    width = len(terms) * DV
    return pl.pallas_call(
        lambda *refs: grads_body(terms, turned, len(lefts), *refs),
        grid=(model // rows,),
        out_shape=pltpu.HBM((model, groups * width), BF),
        in_specs=specs,
        out_specs=pl.BlockSpec((rows, width), lambda i: (i, group)),
        input_output_aliases={} if into is None else {len(arrays) - 1: 0},
        compiler_params=pltpu.CompilerParams(vmem_limit_bytes=20 * 2**20),
        cost_estimate=pl.CostEstimate(
            flops=2 * 512 * model * width, bytes_accessed=2 * model * (width + 512), transcendentals=0
        ),
    )(*arrays)


def norm_body(mine, theirs, gain, bias, out):
    def run(ref):
        values = ref[...].astype(F32)
        centred = values - jnp.mean(values, axis=-1, keepdims=True)
        scaling = lax.rsqrt(jnp.mean(centred * centred, axis=-1, keepdims=True) + 1e-05)
        out[...] = (centred * scaling * gain[...] + bias[...]).astype(BF)

    pl.when(pl.program_id(0) < SIDE)(lambda: run(mine))
    pl.when(pl.program_id(0) >= SIDE)(lambda: run(theirs))


def norm_rows(mine, theirs, gain, bias):
    size, model = mine.shape[0], gain.shape[0]
    part = size // SIDE
    vector = pl.BlockSpec((1, model), lambda i: (0, 0))
    return pl.pallas_call(
        norm_body,
        grid=(2 * SIDE,),
        out_shape=shaped(BF, 2 * size, model),
        in_specs=[
            pl.BlockSpec((part, model), lambda i: (jnp.minimum(i, SIDE - 1), 0)),
            pl.BlockSpec((part, model), lambda i: (jnp.maximum(i - SIDE, 0), 0)),
            vector,
            vector,
        ],
        out_specs=pl.BlockSpec((part, model), lambda i: (i, 0)),
        cost_estimate=pl.CostEstimate(
            flops=20 * size * model, bytes_accessed=12 * size * model, transcendentals=0
        ),
    )(mine, theirs, gain.reshape(1, -1), bias.reshape(1, -1))


def turn_body(rows, out):
    out[...] = rows[...].T


def turned(rows):
    size, model = rows.shape
    return pl.pallas_call(
        turn_body,
        grid=(model // size,),
        out_shape=shaped(rows.dtype, model, size),
        in_specs=[pl.BlockSpec((size, size), lambda i: (0, i))],
        out_specs=pl.BlockSpec((size, size), lambda i: (i, 0)),
        cost_estimate=pl.CostEstimate(
            flops=size * model, bytes_accessed=4 * size * model, transcendentals=0
        ),
    )(rows)


def state_body(x_ref, left, right, *pieces):
    for step, piece in enumerate(pieces):
        width = piece.shape[1]
        part = lax.dot_general(
            left[...],
            lanes(right, head_of(x_ref, -step), width),
            (((0,), (0,)), ((), ())),
            preferred_element_type=F32,
        )
        piece[...] = part.astype(piece.dtype)


def mix_body(weights, *refs):
    count = weights.shape[1]
    for place, out in enumerate(refs[count:]):
        total = 0.0
        for source in range(count):
            total = total + weights[place, source] * refs[source][...].astype(F32)
        out[...] = total.astype(out.dtype)


def quarters_body(x_ref, *refs):
    out = refs[-1]
    for step, piece in enumerate(refs[:-1]):
        width = piece.shape[1]
        start = pl.multiple_of(head_of(x_ref, step) * width, width)
        out[:, pl.ds(start, width)] = piece[...].astype(out.dtype)


def layer_stats(values):
    centred = values - jnp.mean(values, axis=-1, keepdims=True)
    scaling = lax.rsqrt(jnp.mean(centred * centred, axis=-1, keepdims=True) + 1e-05)
    return (centred * scaling, scaling)


def norm_back(grad_hat, normal, scaling):
    return scaling * (
        grad_hat
        - jnp.mean(grad_hat, axis=-1, keepdims=True)
        - normal * jnp.mean(grad_hat * normal, axis=-1, keepdims=True)
    )


def silu_slope(values):
    logistic = jax.nn.sigmoid(values)
    return logistic * (1.0 + values * (1.0 - logistic))


def mm(left, right, left_dim=1, right_dim=0):
    return lax.dot_general(
        left, right, (((left_dim,), (right_dim,)), ((), ())), preferred_element_type=F32
    )


def scan_weights(size, rate, where, backward):
    x, y = where["x"], where["y"]
    steps = jnp.arange(SIDE)

    def mirrored(index):
        return SIDE - 1 - index % SIDE if backward else index % SIDE

    def power(count):
        return jnp.exp(count.astype(F32) * size * rate)

    sources, targets = mirrored(x + steps), mirrored(x - steps)
    lines, line = mirrored(y + steps), mirrored(y)
    to_line = power(SIDE - 1 - sources)
    from_line = jnp.where(lines < line, power(SIDE * jnp.maximum(line - 1 - lines, 0)), 0.0)
    gap = targets[:, None] - 1 - sources[None, :]
    within = jnp.where(gap >= 0, power(jnp.maximum(gap, 0)), 0.0)
    reach = power(targets)[:, None] * from_line[None, 1:]
    return to_line[None, :], jnp.concatenate([within, reach], axis=1)


def scan(left, right, weights, where, beside):
    x = where["x"]
    shape = (left.shape[1], right.shape[1] // SIDE)
    pieces = whole(state_body, [shaped(F32, *shape)] + [shaped(BF, *shape)] * 3, x, left, right)
    got = [pieces[0]] + [hop(pieces[step], "x", step) for step in (1, 2, 3)]
    (total,) = whole(mix_body, [shaped(BF, *shape)], weights[0], *got)
    others = [hop(total, "y", step) for step in (1, 2, 3)]
    given = whole(mix_body, [shaped(BF, *shape)] * SIDE, weights[1], *got, *others)
    moved = [given[0]] + [hop(given[step], "x", step) for step in (1, 2, 3)]
    if beside is not None:
        moved[1], beside = lax.optimization_barrier((moved[1], beside))
    (joined,) = whole(quarters_body, [near(BF, shape[0], right.shape[1])], x, *moved)
    return joined, beside


def project_body(rows_in, weight_in, *refs):
    tables_in, (query, key, value, key_left) = refs[:3], refs[3:7]
    rows, weight, *tables, sems = refs[7:]
    width = weight.shape[1]
    depth = weight.shape[0] // SIDE
    copies = []
    for step in range(SIDE):
        part = pl.ds(step * depth, depth)
        source = weight_in.at[part, pl.ds(0, width)]
        copies.append(pltpu.make_async_copy(source, weight.at[part], sems.at[2 * step]))
        source = rows_in.at[:, part]
        copies.append(pltpu.make_async_copy(source, rows.at[:, part], sems.at[2 * step + 1]))
    for place, (source, table) in enumerate(zip(tables_in, tables)):
        copies.append(pltpu.make_async_copy(source, table, sems.at[2 * SIDE + place]))
    for copy in copies:
        copy.start()
    total = 0.0
    for step in range(SIDE):
        copies[2 * step].wait()
        copies[2 * step + 1].wait()
        part = slice(step * depth, (step + 1) * depth)
        total = total + jnp.dot(rows[:, part], weight[part, :], preferred_element_type=F32)
    for copy in copies[2 * SIDE :]:
        copy.wait()
    cosine, sine, left_over = tables
    half = DK // 2
    for place in range(2):
        a = total[:, place * DK : place * DK + half]
        b = total[:, place * DK + half : (place + 1) * DK]
        turned_halves = (a * cosine[...] - b * sine[...], b * cosine[...] + a * sine[...])
        for index, turned_half in enumerate(turned_halves):
            columns = slice(index * half, (index + 1) * half)
            if place == 0:
                query[:, columns] = turned_half.astype(BF)
            else:
                key[:, columns] = (turned_half * DK ** (-0.5)).astype(BF)
                key_left[:, columns] = (key[:, columns].astype(F32) * left_over[...]).astype(BF)
    value[...] = total[:, 2 * DK :].astype(BF)


def project(rows, weight, cosine, sine, leftover):
    size, model = rows.shape
    vmem = pl.BlockSpec(memory_space=pltpu.VMEM)
    kept = pl.BlockSpec(memory_space=pl.ANY)
    steps = 2 + DV // DK
    return pl.pallas_call(
        project_body,
        out_shape=[
            near(BF, size, DK),
            near(BF, size, DK),
            near(BF, size, DV),
            near(BF, size, DK),
        ],
        in_specs=[kept] * 5,
        out_specs=[vmem] * 4,
        scratch_shapes=[
            pltpu.VMEM((size, model), BF),
            pltpu.VMEM((model, steps * DK), BF),
            *[pltpu.VMEM(table.shape, F32) for table in (cosine, sine, leftover)],
            pltpu.SemaphoreType.DMA((2 * SIDE + 3,)),
        ],
        compiler_params=pltpu.CompilerParams(vmem_limit_bytes=20 * 2**20),
        cost_estimate=pl.CostEstimate(
            flops=2 * size * model * steps * DK, bytes_accessed=2 * model * steps * DK, transcendentals=0
        ),
    )(
        *[
            pltpu.with_memory_space_constraint(array, pltpu.HBM)
            for array in (rows, weight, cosine, sine, leftover)
        ]
    )


def feed_back_body(z_ref, first, second, weights, *outs):
    for rows, out in zip((first, second), outs):
        out[...] = jnp.dot(rows[...], weights[:, 2 * DV :], preferred_element_type=F32)


def feed_body(z_ref, mine, theirs, back_mine, back_theirs, weights, *outs):
    inner, grad_gate, grad_up, share = outs
    gate, up = weights[:, :DV], weights[:, DV : 2 * DV]
    size = mine.shape[0]
    for place, (rows, grad_inner) in enumerate(((theirs, back_theirs), (mine, back_mine))):
        gate_pre = jnp.dot(rows[...], gate, preferred_element_type=F32)
        upward = jnp.dot(rows[...], up, preferred_element_type=F32)
        logistic = jax.nn.sigmoid(gate_pre)
        gate_act = gate_pre * logistic
        slope = logistic * (1.0 + gate_pre * (1.0 - logistic))
        one = (grad_inner[...] * upward * slope).astype(BF)
        two = (grad_inner[...] * gate_act).astype(BF)
        kept = slice((1 - place) * size, (2 - place) * size)
        inner[kept, :] = (gate_act * upward).astype(BF)
        grad_gate[kept, :] = one
        grad_up[kept, :] = two
        if place == 0:
            share[...] = (mm(one, gate, 1, 1) + mm(two, up, 1, 1)).astype(BF)


def feed_pair_body(z_ref, grad_gate, grad_up, weights, received, *outs):
    height = outs[0].shape[0]
    rows = slice(0, SIDE * height)
    own = mm(grad_gate[rows, :], weights[:, :DV], 1, 1)
    own = own + mm(grad_up[rows, :], weights[:, DV : 2 * DV], 1, 1)
    for step, out in enumerate(outs):
        rows = slice(step * height, (step + 1) * height)
        out[...] = (own[rows] + received[rows, :].astype(F32)).astype(out.dtype)


def feed_out_body(inner, weight, own, other):
    size = own.shape[0]
    own[...] = mm(inner[:size, :], weight[...], 1, 1)
    other[...] = mm(inner[size:, :], weight[...], 1, 1).astype(BF)


def feed_out_shares(inner, weights):
    size, model = inner.shape[0] // 2, weights.shape[0]
    return pl.pallas_call(
        feed_out_body,
        grid=(model // DV,),
        out_shape=[shaped(F32, size, model), shaped(BF, size, 2 * model)],
        in_specs=[
            pl.BlockSpec(inner.shape, lambda i: (0, 0)),
            pl.BlockSpec((DV, DV), lambda i: (i, 2)),
        ],
        out_specs=[
            pl.BlockSpec((size, DV), lambda i: (0, i)),
            pl.BlockSpec((size, DV), lambda i: (0, i + model // DV)),
        ],
        compiler_params=pltpu.CompilerParams(vmem_limit_bytes=16 * 2**20),
        cost_estimate=pl.CostEstimate(
            flops=4 * size * model * DV, bytes_accessed=10 * size * model, transcendentals=0
        ),
    )(inner, pltpu.with_memory_space_constraint(weights, pltpu.HBM))


def last_share_body(qk, value, swish, qk_w, value_w, swish_w, kept, own, other):
    share = mm(qk[...], qk_w[...], 1, 1) + mm(value[...], value_w[...], 1, 1)
    share = share + mm(swish[...], swish_w[...], 1, 1)
    size = own.shape[0]
    own[...] = share[:size]
    other[...] = share[size:].astype(BF)


def last_share(rights, weights, joint):
    count, model = rights[0].shape[0], weights.shape[0]
    size = count // 2
    fixed = pl.BlockSpec((count, DV), lambda i: (0, 0))
    return pl.pallas_call(
        last_share_body,
        grid=(model // DV,),
        out_shape=[shaped(F32, size, model), shaped(BF, size, 2 * model)],
        in_specs=[fixed] * 3
        + [pl.BlockSpec((DV, DV), lambda i, j=j: (i, j)) for j in range(3)]
        + [pl.BlockSpec(memory_space=pl.ANY)],
        out_specs=[pl.BlockSpec((size, DV), lambda i: (0, i))] * 2,
        input_output_aliases={6: 1},
        compiler_params=pltpu.CompilerParams(vmem_limit_bytes=16 * 2**20),
        cost_estimate=pl.CostEstimate(
            flops=6 * count * model * DV, bytes_accessed=14 * count * model, transcendentals=0
        ),
    )(*rights, *[pltpu.with_memory_space_constraint(weights, pltpu.HBM)] * 3, joint)


def pair_body(z_ref, *refs):
    owns, received, outs = refs[: -SIDE - 1], refs[-SIDE - 1], refs[-SIDE:]
    height = outs[0].shape[0]
    for step, out in enumerate(outs):
        rows = slice(step * height, (step + 1) * height)
        column = 0
        for ref in owns:
            columns = slice(column, column + ref.shape[1])
            out[:, columns] = (ref[rows, :] + received[rows, columns].astype(F32)).astype(out.dtype)
            column += ref.shape[1]


def reduce_line(values, axis, dim, where):
    here = where[axis]
    total = block(values, here, dim)
    for step in (1, 2, 3):
        total = total + hop(block(values, here - step, dim), axis, step)
    return total


def local(
    tokens,
    mixer_gain,
    mixer_bias,
    query_weight,
    key_weight,
    value_weight,
    swish_weight,
    output_weight,
    feed_gain,
    feed_bias,
    gate_weight,
    up_weight,
    down_weight,
    cotangent,
):
    place = lax.axis_index("seq")
    where = {"y": place // 16, "x": place // 4 % 4, "z": place % 4}
    z, t = where["z"], lax.axis_index("tp")
    rows = tokens.shape[0]
    half = rows // 2
    shard = query_weight.shape[0]
    planes = [[16 * b + 4 * a + c for b in range(4) for a in range(4)] for c in range(4)]

    def own(values):
        return lax.dynamic_slice_in_dim(values, t * half, half, 0)

    pieces = pack(
        z,
        [
            query_weight,
            key_weight,
            value_weight,
            swish_weight,
            output_weight,
            gate_weight,
            up_weight,
            down_weight,
        ],
    )

    def gathered(parts):
        moved = [parts[0]] + [hop(parts[step], "z", step) for step in (1, 2, 3)]
        (share,) = whole(
            assemble_body, [jax.ShapeDtypeStruct((rows, parts[0].shape[1]), BF)], z, *moved
        )
        return share

    mixer_share = gathered(pieces[:SIDE])
    mixer_full = lax.all_gather(mixer_share, "seq", axis_index_groups=planes, axis=0, tiled=True)
    feed_share = gathered(pieces[SIDE:])
    tokens_own, upstream_own = own(tokens), own(cotangent)
    model = tokens.shape[1]
    both_mine, both_theirs, _ = gather_rows(jnp.concatenate([tokens_own, upstream_own], axis=1))
    upstream_mine, upstream_theirs = both_mine[:, model:], both_theirs[:, model:]
    normed = norm_rows(both_mine, both_theirs, mixer_gain, mixer_bias)
    normed_turned = turned(normed)

    number = jnp.arange(SIDE * rows)
    local_place = (
        ((z + number // half % SIDE) % SIDE) * rows
        + ((t + number // (SIDE * half)) % 2) * half
        + number % half
    )
    count = SIDE * rows
    positions = ((place // SIDE) * count + local_place).astype(F32)
    frequency = 1.0 / 10000.0 ** jnp.linspace(0.0, 1.0, DK // 2, dtype=F32)
    phases = positions[:, None] * frequency[None, :]
    cosine, sine = jnp.cos(phases), jnp.sin(phases)

    def turn(values):
        a, b = values[:, : DK // 2], values[:, DK // 2 :]
        return jnp.concatenate([a * cosine - b * sine, b * cosine + a * sine], axis=1)

    def turn_back(values):
        a, b = values[:, : DK // 2], values[:, DK // 2 :]
        return jnp.concatenate([a * cosine + b * sine, b * cosine - a * sine], axis=1)

    rate = jnp.log(1.0 - 2.0 ** (-5.0 - (SIDE * t + z).astype(F32)))
    places = local_place.astype(F32)
    offsets = places[:, None] - places[None, :]
    within = jnp.where(offsets >= 0, jnp.exp(jnp.maximum(offsets, 0.0) * rate), 0.0)
    onward = jnp.exp(places * rate)[:, None]
    leftover = jnp.exp((count - places) * rate)[:, None]

    weights = [scan_weights(count, rate, where, backward) for backward in (False, True)]
    early = (
        feed_share,
        normed,
        normed_turned,
        upstream_mine,
        upstream_theirs,
        cosine,
        sine,
        within,
        leftover,
        onward,
        weights,
    )
    (
        feed_share,
        normed,
        normed_turned,
        upstream_mine,
        upstream_theirs,
        cosine,
        sine,
        within,
        leftover,
        onward,
        weights,
    ) = lax.optimization_barrier(early)
    feed_full = lax.all_gather(feed_share, "seq", axis_index_groups=planes, axis=0, tiled=True)
    query, key, value, key_left = project(normed, mixer_full, cosine, sine, leftover)
    mixer_rest, value = lax.optimization_barrier((mixer_full, value))
    sw_full, out_full = lax.optimization_barrier(
        (mixer_rest[:, 2 * DV : 3 * DV], mixer_rest[:, 3 * DV :])
    )
    incoming, switch = scan(key_left, value, weights[0], where, mm(normed, sw_full))
    scores = (mm(query, key, 1, 1) * within).astype(BF)
    retained = mm(scores, value) + mm(query, incoming) * onward
    normal_ret, scale_ret = layer_stats(retained)
    swish_act = jax.nn.silu(switch)
    branch = (swish_act * normal_ret).astype(BF)
    part = branch.shape[0] // 2
    shares_one = ring_shares(
        mm(branch[:part], out_full, 1, 1), mm(branch[part:], out_full, 1, 1), z
    )
    grad_inner = whole(
        feed_back_body,
        [shaped(F32, part, DV)] * 2,
        z,
        upstream_mine,
        upstream_theirs,
        feed_full,
        flops=4 * part * upstream_mine.shape[1] * DV,
    )
    attended = total_of(shares_one)

    residual_in = tokens_own.astype(F32)
    residual = residual_in + attended
    normal_two, scale_two = layer_stats(residual)
    *normed_two, grad_inner = gather_rows(
        (normal_two * feed_gain + feed_bias).astype(BF), grad_inner
    )
    inner_act, grad_gate, grad_up, other_share = whole(
        feed_body,
        [near(BF, count, DV)] * 3 + [near(BF, part, model)],
        z,
        *normed_two,
        *grad_inner,
        feed_full,
        flops=16 * part * model * DV,
    )
    halves = (slice(0, part), slice(part, count))
    feed_terms = grads(
        [[(0, 0), (1, 1)], [(0, 2), (1, 3)], [(2, 4), (3, 5)]],
        [*normed_two, upstream_mine, upstream_theirs],
        [],
        [array[rows_half] for array in (grad_gate, grad_up, inner_act) for rows_half in halves],
    )
    received = swap(other_share)
    received, feed_terms = lax.optimization_barrier((received, feed_terms))
    pair_two = whole(
        feed_pair_body,
        [shaped(F32, half, model)] + [shaped(BF, half, model)] * 3,
        z,
        grad_gate,
        grad_up,
        feed_full,
        received,
    )
    shares_two = [pair_two[0]] + [hop(pair_two[step], "z", -step) for step in (1, 2, 3)]
    feed_sum = lax.psum_scatter(
        feed_terms, "seq", axis_index_groups=planes, scatter_dimension=0, tiled=True
    )
    grad_norm_two = total_of(shares_two)
    upstream = upstream_own.astype(F32)
    grad_resid = upstream + norm_back(grad_norm_two * feed_gain, normal_two, scale_two)
    *grad_attended, _ = gather_rows(grad_resid.astype(BF))

    grad_branch = jnp.concatenate([mm(rows_half, out_full) for rows_half in grad_attended], axis=0)
    grad_switch = (grad_branch * normal_ret * silu_slope(switch)).astype(BF)
    grad_low = norm_back(grad_branch * swish_act, normal_ret, scale_ret).astype(BF)
    grad_onward = (grad_low.astype(F32) * onward).astype(BF)
    early_terms = grads(
        [[(0, 0)], [(1, 1), (2, 2)]],
        [normed_turned, *grad_attended],
        [0],
        [grad_switch, branch[:part], branch[part:]],
        2,
        0,
    )
    outgoing, _ = scan(query, grad_onward, weights[1], where, None)
    grad_scores = (mm(grad_low, value, 1, 1) * within).astype(BF)
    grad_query = mm(grad_scores, key) + mm(grad_onward, incoming, 1, 1)
    grad_key = mm(grad_scores, query, 0, 0) + mm(value, outgoing, 1, 1) * leftover
    grad_value = mm(scores, grad_low, 0, 0) + mm(key_left, outgoing)
    query_grads = turn_back(grad_query).astype(BF)
    key_grads = (turn_back(grad_key) * DK ** (-0.5)).astype(BF)
    qk_grads = jnp.concatenate([query_grads, key_grads], axis=1)
    value_grads = grad_value.astype(BF)

    mixer_terms = grads(
        [[(0, 0)], [(0, 1)]], [normed_turned], [0], [qk_grads, value_grads], 2, 1, early_terms
    )
    mixer_terms, feed_sum = lax.optimization_barrier((mixer_terms, feed_sum))
    mixer_sum = lax.psum_scatter(
        mixer_terms, "seq", axis_index_groups=planes, scatter_dimension=0, tiled=True
    )

    mixer_terms, qk_grads, value_grads, grad_switch, inner_act = lax.optimization_barrier(
        (mixer_terms, qk_grads, value_grads, grad_switch, inner_act)
    )
    feed_own, joint = feed_out_shares(inner_act, feed_full)
    share_own, joint = last_share([qk_grads, value_grads, grad_switch], mixer_full, joint)
    joint_pair = whole(
        pair_body,
        [shaped(F32, half, 2 * model)] + [shaped(BF, half, 2 * model)] * 3,
        z,
        share_own,
        feed_own,
        swap(joint),
    )
    joint_total = total_of(
        [joint_pair[0]] + [hop(joint_pair[step], "z", -step) for step in (1, 2, 3)]
    )
    grad_norm_one = joint_total[:, :model]
    block_output = (residual + joint_total[:, model:]).astype(BF)
    normal_own, scale_own = layer_stats(residual_in)
    tokens_grad = grad_resid + norm_back(grad_norm_one * mixer_gain, normal_own, scale_own)
    norms = jnp.stack(
        [
            jnp.sum(grad_norm_one * normal_own, axis=0),
            jnp.sum(grad_norm_one, axis=0),
            jnp.sum(grad_norm_two * normal_two, axis=0),
            jnp.sum(grad_norm_two, axis=0),
        ]
    )
    norms = norms.reshape(4, SIDE, SIDE, SIDE, -1).transpose(1, 2, 3, 0, 4)
    norms = norms.reshape(SIDE, SIDE, SIDE, -1)
    for axis, dim in (("x", 1), ("y", 0), ("z", 0)):
        norms = reduce_line(norms, axis, dim, where)
    norms = norms.reshape(1, -1)
    norms = (norms + swap(norms)).reshape(4, -1)

    def cut_rows(summed):
        return whole(cut_body, [shaped(BF, shard, summed.shape[1])] * SIDE, z, summed)

    def returned(parts, widths, paired):
        moved = [parts[0]] + [hop(parts[step], "z", step) for step in (1, 2, 3)]
        outs = [shaped(F32, shard, SIDE * width) for width in widths]
        return whole(lambda *refs: unpack_body(paired, *refs), outs, z, *moved)

    gate_sum, up_sum, down_sum = returned(cut_rows(feed_sum), [DV] * 3, ())
    swish_sum, output_sum, query_sum, key_sum, value_sum = returned(
        cut_rows(mixer_sum), [DV, DV, DK, DK, DV], (2, 3)
    )

    def both_halves(values):
        theirs = swap(values)
        return jnp.concatenate(
            [jnp.where(t == 0, values, theirs), jnp.where(t == 0, theirs, values)], axis=0
        )

    return (
        both_halves(block_output),
        both_halves(tokens_grad),
        norms[0],
        norms[1],
        query_sum,
        key_sum,
        value_sum,
        swish_sum,
        output_sum,
        norms[2],
        norms[3],
        gate_sum,
        up_sum,
        down_sum,
    )


def solution(mesh):
    split = P("seq", "tp")
    token = P("seq", None)
    in_specs = (token, P(), P()) + (split,) * 5 + (P(), P()) + (split,) * 3 + (token,)
    out_specs = (token, token, P("seq"), P("seq")) + (split,) * 5 + (P("seq"), P("seq")) + (split,) * 3
    return jax.shard_map(local, mesh=mesh, in_specs=in_specs, out_specs=out_specs, check_vma=False)
```

```python
import jax
import jax.numpy as jnp
from jax import lax
from jax.experimental import pallas as pl
from jax.experimental.pallas import tpu as pltpu
from jax.sharding import PartitionSpec as P

DK = 256
DV = 512
SIDE = 4
BF = jnp.bfloat16
F32 = jnp.float32
STRIDE = {"y": 16, "x": 4, "z": 1}


def pairs(axis, step):
    table = []
    for source in range(64):
        place = source // STRIDE[axis] % SIDE
        target = source + ((place - step) % SIDE - place) * STRIDE[axis]
        table.append((source, target))
    return table


def hop(value, axis, step):
    return lax.ppermute(value, "seq", pairs(axis, step % SIDE))


def swap(value):
    return lax.ppermute(value, "tp", [(0, 1), (1, 0)])


def direct(value, axis):
    return [value] + [hop(value, axis, step) for step in (1, 2, 3)]


def block(values, index, axis=0):
    return lax.dynamic_index_in_dim(values, index % SIDE, axis, keepdims=False)


def gather_rows(rows, beside=None):
    parts = direct(rows, "z")
    if beside is not None:
        parts[1], beside = lax.optimization_barrier((parts[1], beside))
    mine = jnp.concatenate(parts, axis=0)
    return (mine, swap(mine), beside)


def ring_shares(own, other, z):
    height, model = own.shape[0] // SIDE, own.shape[1]
    pair = whole(
        pair_body,
        [shaped(F32, height, model)] + [shaped(BF, height, model)] * 3,
        z,
        own,
        swap(other.astype(BF)),
    )
    return [pair[0]] + [hop(pair[step], "z", -step) for step in (1, 2, 3)]


def total_of(shares):
    return sum(share.astype(F32) for share in shares[1:]) + shares[0]


def whole(body, outs, scalars, *arrays, flops=0):
    vmem = pl.BlockSpec(memory_space=pltpu.VMEM)
    moved = sum(array.size * array.dtype.itemsize for array in arrays)
    if scalars.ndim == 0:
        scalars = scalars.reshape(1).astype(jnp.int32)
    return pl.pallas_call(
        body,
        out_shape=outs,
        in_specs=[pl.BlockSpec(memory_space=pltpu.SMEM)] + [vmem] * len(arrays),
        out_specs=[vmem] * len(outs),
        compiler_params=pltpu.CompilerParams(vmem_limit_bytes=16 * 2**20),
        cost_estimate=pl.CostEstimate(flops=flops, bytes_accessed=moved, transcendentals=0),
    )(scalars, *arrays)


def near(dtype, *shape):
    return pltpu.VMEM(shape, dtype)


def shaped(dtype, *shape):
    return jax.ShapeDtypeStruct(shape, dtype)


def head_of(z_ref, step):
    return lax.rem(z_ref[0] + SIDE + step, SIDE)


def lanes(ref, head, width):
    return ref[:, pl.ds(pl.multiple_of(head * width, width), width)]


def pack_body(z_ref, *refs):
    sources, pieces = refs[:8], refs[8 : 8 + 2 * SIDE]
    held, sems = refs[8 + 2 * SIDE : -1], refs[-1]
    copies = [
        pltpu.make_async_copy(source, ref, sems.at[place])
        for place, (source, ref) in enumerate(zip(sources, held))
    ]
    for copy in copies:
        copy.start()
    old = lax.broadcasted_iota(jnp.int32, (DK, DK), 0)
    new = lax.broadcasted_iota(jnp.int32, (DK, DK), 1)
    shuffle = (old == jnp.where(new < DK // 2, 2 * new, 2 * new - DK + 1)).astype(F32).astype(BF)
    for place, ref in enumerate(held):
        copies[place].wait()
        for step in range(SIDE):
            head = head_of(z_ref, -step)
            if place < 2:
                part = jnp.dot(lanes(ref, head, DK), shuffle, preferred_element_type=F32)
                pieces[step][:, place * DK : (place + 1) * DK] = part.astype(BF)
            elif place < 5:
                pieces[step][:, (place - 1) * DV : place * DV] = lanes(ref, head, DV)
            else:
                pieces[SIDE + step][:, (place - 5) * DV : (place - 4) * DV] = lanes(ref, head, DV)


def pack(z, weights):
    vmem = pl.BlockSpec(memory_space=pltpu.VMEM)
    shard = weights[0].shape[0]
    outs = [jax.ShapeDtypeStruct((shard, 2 * DK + 3 * DV), BF)] * SIDE
    outs = outs + [jax.ShapeDtypeStruct((shard, 3 * DV), BF)] * SIDE
    return pl.pallas_call(
        pack_body,
        out_shape=outs,
        in_specs=[pl.BlockSpec(memory_space=pltpu.SMEM)]
        + [pl.BlockSpec(memory_space=pl.ANY)] * len(weights),
        out_specs=[vmem] * len(outs),
        scratch_shapes=[pltpu.VMEM(weight.shape, BF) for weight in weights]
        + [pltpu.SemaphoreType.DMA((len(weights),))],
        compiler_params=pltpu.CompilerParams(vmem_limit_bytes=16 * 2**20),
    )(
        z.reshape(1).astype(jnp.int32),
        *[pltpu.with_memory_space_constraint(weight, pltpu.HBM) for weight in weights],
    )


def cut_body(z_ref, whole_ref, *pieces):
    height = pieces[0].shape[0]
    for step, piece in enumerate(pieces):
        row = pl.multiple_of(head_of(z_ref, -step) * height, height)
        piece[...] = whole_ref[pl.ds(row, height), :]


def unpack_body(paired, z_ref, *refs):
    outs = refs[SIDE:]
    old = lax.broadcasted_iota(jnp.int32, (DK, DK), 1)
    new = lax.broadcasted_iota(jnp.int32, (DK, DK), 0)
    shuffle = (old == jnp.where(new < DK // 2, 2 * new, 2 * new - DK + 1)).astype(F32).astype(BF)
    for step in range(SIDE):
        piece = refs[step]
        head = head_of(z_ref, step)
        start = 0
        for place, out in enumerate(outs):
            width = out.shape[1] // SIDE
            part = piece[:, start : start + width]
            if place in paired:
                part = jnp.dot(part, shuffle, preferred_element_type=F32)
            out[:, pl.ds(pl.multiple_of(head * width, width), width)] = part.astype(F32)
            start += width


def assemble_body(z_ref, *refs):
    for step in range(SIDE):
        piece = refs[step]
        height = piece.shape[0]
        row = pl.multiple_of(head_of(z_ref, step) * height, height)
        column = 0
        for whole_ref in refs[SIDE:]:
            width = whole_ref.shape[1]
            whole_ref[pl.ds(row, height), :] = piece[:, column : column + width]
            column += width


def grads_body(terms, turned, lefts, *refs):
    left, right, out = refs[:lefts], refs[lefts : lefts + terms[-1][-1][1] + 1], refs[-1]
    for place, term in enumerate(terms):
        part = 0.0
        for a, b in term:
            part = part + mm(left[a][...], right[b][...], int(a in turned), 0)
        out[:, place * DV : (place + 1) * DV] = part.astype(BF)


def grads(terms, lefts, turned, rights, groups=1, group=0, into=None, rows=512):
    model = lefts[0].shape[0 if 0 in turned else 1]
    specs = [
        pl.BlockSpec((rows, left.shape[1]), lambda i: (i, 0))
        if place in turned
        else pl.BlockSpec((left.shape[0], rows), lambda i: (0, i))
        for place, left in enumerate(lefts)
    ]
    specs = specs + [pl.BlockSpec(right.shape, lambda i: (0, 0)) for right in rights]
    arrays = [*lefts, *rights]
    if into is not None:
        specs.append(pl.BlockSpec(memory_space=pl.ANY))
        arrays.append(into)
    width = len(terms) * DV
    return pl.pallas_call(
        lambda *refs: grads_body(terms, turned, len(lefts), *refs),
        grid=(model // rows,),
        out_shape=pltpu.HBM((model, groups * width), BF),
        in_specs=specs,
        out_specs=pl.BlockSpec((rows, width), lambda i: (i, group)),
        input_output_aliases={} if into is None else {len(arrays) - 1: 0},
        compiler_params=pltpu.CompilerParams(vmem_limit_bytes=20 * 2**20),
        cost_estimate=pl.CostEstimate(
            flops=2 * 512 * model * width, bytes_accessed=2 * model * (width + 512), transcendentals=0
        ),
    )(*arrays)


def norm_body(mine, theirs, gain, bias, out):
    def run(ref):
        values = ref[...].astype(F32)
        centred = values - jnp.mean(values, axis=-1, keepdims=True)
        scaling = lax.rsqrt(jnp.mean(centred * centred, axis=-1, keepdims=True) + 1e-05)
        out[...] = (centred * scaling * gain[...] + bias[...]).astype(BF)

    pl.when(pl.program_id(0) < SIDE)(lambda: run(mine))
    pl.when(pl.program_id(0) >= SIDE)(lambda: run(theirs))


def norm_rows(mine, theirs, gain, bias):
    size, model = mine.shape[0], gain.shape[0]
    part = size // SIDE
    vector = pl.BlockSpec((1, model), lambda i: (0, 0))
    return pl.pallas_call(
        norm_body,
        grid=(2 * SIDE,),
        out_shape=shaped(BF, 2 * size, model),
        in_specs=[
            pl.BlockSpec((part, model), lambda i: (jnp.minimum(i, SIDE - 1), 0)),
            pl.BlockSpec((part, model), lambda i: (jnp.maximum(i - SIDE, 0), 0)),
            vector,
            vector,
        ],
        out_specs=pl.BlockSpec((part, model), lambda i: (i, 0)),
        cost_estimate=pl.CostEstimate(
            flops=20 * size * model, bytes_accessed=12 * size * model, transcendentals=0
        ),
    )(mine, theirs, gain.reshape(1, -1), bias.reshape(1, -1))


def turn_body(rows, out):
    out[...] = rows[...].T


def turned(rows):
    size, model = rows.shape
    return pl.pallas_call(
        turn_body,
        grid=(model // size,),
        out_shape=shaped(rows.dtype, model, size),
        in_specs=[pl.BlockSpec((size, size), lambda i: (0, i))],
        out_specs=pl.BlockSpec((size, size), lambda i: (i, 0)),
        cost_estimate=pl.CostEstimate(
            flops=size * model, bytes_accessed=4 * size * model, transcendentals=0
        ),
    )(rows)


def state_body(x_ref, left, right, *pieces):
    for step, piece in enumerate(pieces):
        width = piece.shape[1]
        part = lax.dot_general(
            left[...],
            lanes(right, head_of(x_ref, -step), width),
            (((0,), (0,)), ((), ())),
            preferred_element_type=F32,
        )
        piece[...] = part.astype(piece.dtype)


def mix_body(weights, *refs):
    count = weights.shape[1]
    for place, out in enumerate(refs[count:]):
        total = 0.0
        for source in range(count):
            total = total + weights[place, source] * refs[source][...].astype(F32)
        out[...] = total.astype(out.dtype)


def quarters_body(x_ref, *refs):
    out = refs[-1]
    for step, piece in enumerate(refs[:-1]):
        width = piece.shape[1]
        start = pl.multiple_of(head_of(x_ref, step) * width, width)
        out[:, pl.ds(start, width)] = piece[...].astype(out.dtype)


def layer_stats(values):
    centred = values - jnp.mean(values, axis=-1, keepdims=True)
    scaling = lax.rsqrt(jnp.mean(centred * centred, axis=-1, keepdims=True) + 1e-05)
    return (centred * scaling, scaling)


def norm_back(grad_hat, normal, scaling):
    return scaling * (
        grad_hat
        - jnp.mean(grad_hat, axis=-1, keepdims=True)
        - normal * jnp.mean(grad_hat * normal, axis=-1, keepdims=True)
    )


def silu_slope(values):
    logistic = jax.nn.sigmoid(values)
    return logistic * (1.0 + values * (1.0 - logistic))


def mm(left, right, left_dim=1, right_dim=0):
    return lax.dot_general(
        left, right, (((left_dim,), (right_dim,)), ((), ())), preferred_element_type=F32
    )


def scan_weights(size, rate, where, backward):
    x, y = where["x"], where["y"]
    steps = jnp.arange(SIDE)

    def mirrored(index):
        return SIDE - 1 - index % SIDE if backward else index % SIDE

    def power(count):
        return jnp.exp(count.astype(F32) * size * rate)

    sources, targets = mirrored(x + steps), mirrored(x - steps)
    lines, line = mirrored(y + steps), mirrored(y)
    to_line = power(SIDE - 1 - sources)
    from_line = jnp.where(lines < line, power(SIDE * jnp.maximum(line - 1 - lines, 0)), 0.0)
    gap = targets[:, None] - 1 - sources[None, :]
    within = jnp.where(gap >= 0, power(jnp.maximum(gap, 0)), 0.0)
    reach = power(targets)[:, None] * from_line[None, 1:]
    return to_line[None, :], jnp.concatenate([within, reach], axis=1)


def scan(left, right, weights, where, beside):
    x = where["x"]
    shape = (left.shape[1], right.shape[1] // SIDE)
    pieces = whole(state_body, [shaped(F32, *shape)] + [shaped(BF, *shape)] * 3, x, left, right)
    got = [pieces[0]] + [hop(pieces[step], "x", step) for step in (1, 2, 3)]
    (total,) = whole(mix_body, [shaped(BF, *shape)], weights[0], *got)
    others = [hop(total, "y", step) for step in (1, 2, 3)]
    given = whole(mix_body, [shaped(BF, *shape)] * SIDE, weights[1], *got, *others)
    moved = [given[0]] + [hop(given[step], "x", step) for step in (1, 2, 3)]
    if beside is not None:
        moved[1], beside = lax.optimization_barrier((moved[1], beside))
    (joined,) = whole(quarters_body, [near(BF, shape[0], right.shape[1])], x, *moved)
    return joined, beside


def project_body(rows_in, weight_in, *refs):
    tables_in, (query, key, value, key_left) = refs[:3], refs[3:7]
    rows, weight, *tables, sems = refs[7:]
    width = weight.shape[1]
    depth = weight.shape[0] // SIDE
    copies = []
    for step in range(SIDE):
        part = pl.ds(step * depth, depth)
        source = weight_in.at[part, pl.ds(0, width)]
        copies.append(pltpu.make_async_copy(source, weight.at[part], sems.at[2 * step]))
        source = rows_in.at[:, part]
        copies.append(pltpu.make_async_copy(source, rows.at[:, part], sems.at[2 * step + 1]))
    for place, (source, table) in enumerate(zip(tables_in, tables)):
        copies.append(pltpu.make_async_copy(source, table, sems.at[2 * SIDE + place]))
    for copy in copies:
        copy.start()
    total = 0.0
    for step in range(SIDE):
        copies[2 * step].wait()
        copies[2 * step + 1].wait()
        part = slice(step * depth, (step + 1) * depth)
        total = total + jnp.dot(rows[:, part], weight[part, :], preferred_element_type=F32)
    for copy in copies[2 * SIDE :]:
        copy.wait()
    cosine, sine, left_over = tables
    half = DK // 2
    for place in range(2):
        a = total[:, place * DK : place * DK + half]
        b = total[:, place * DK + half : (place + 1) * DK]
        turned_halves = (a * cosine[...] - b * sine[...], b * cosine[...] + a * sine[...])
        for index, turned_half in enumerate(turned_halves):
            columns = slice(index * half, (index + 1) * half)
            if place == 0:
                query[:, columns] = turned_half.astype(BF)
            else:
                key[:, columns] = (turned_half * DK ** (-0.5)).astype(BF)
                key_left[:, columns] = (key[:, columns].astype(F32) * left_over[...]).astype(BF)
    value[...] = total[:, 2 * DK :].astype(BF)


def project(rows, weight, cosine, sine, leftover):
    size, model = rows.shape
    vmem = pl.BlockSpec(memory_space=pltpu.VMEM)
    kept = pl.BlockSpec(memory_space=pl.ANY)
    steps = 2 + DV // DK
    return pl.pallas_call(
        project_body,
        out_shape=[
            near(BF, size, DK),
            near(BF, size, DK),
            near(BF, size, DV),
            near(BF, size, DK),
        ],
        in_specs=[kept] * 5,
        out_specs=[vmem] * 4,
        scratch_shapes=[
            pltpu.VMEM((size, model), BF),
            pltpu.VMEM((model, steps * DK), BF),
            *[pltpu.VMEM(table.shape, F32) for table in (cosine, sine, leftover)],
            pltpu.SemaphoreType.DMA((2 * SIDE + 3,)),
        ],
        compiler_params=pltpu.CompilerParams(vmem_limit_bytes=20 * 2**20),
        cost_estimate=pl.CostEstimate(
            flops=2 * size * model * steps * DK, bytes_accessed=2 * model * steps * DK, transcendentals=0
        ),
    )(
        *[
            pltpu.with_memory_space_constraint(array, pltpu.HBM)
            for array in (rows, weight, cosine, sine, leftover)
        ]
    )


def feed_back_body(z_ref, first, second, weights, *outs):
    for rows, out in zip((first, second), outs):
        out[...] = jnp.dot(rows[...], weights[:, 2 * DV :], preferred_element_type=F32)


def feed_body(z_ref, mine, theirs, back_mine, back_theirs, weights, *outs):
    inner, grad_gate, grad_up, share = outs
    gate, up = weights[:, :DV], weights[:, DV : 2 * DV]
    size = mine.shape[0]
    for place, (rows, grad_inner) in enumerate(((theirs, back_theirs), (mine, back_mine))):
        gate_pre = jnp.dot(rows[...], gate, preferred_element_type=F32)
        upward = jnp.dot(rows[...], up, preferred_element_type=F32)
        logistic = jax.nn.sigmoid(gate_pre)
        gate_act = gate_pre * logistic
        slope = logistic * (1.0 + gate_pre * (1.0 - logistic))
        one = (grad_inner[...] * upward * slope).astype(BF)
        two = (grad_inner[...] * gate_act).astype(BF)
        kept = slice((1 - place) * size, (2 - place) * size)
        inner[kept, :] = (gate_act * upward).astype(BF)
        grad_gate[kept, :] = one
        grad_up[kept, :] = two
        if place == 0:
            share[...] = (mm(one, gate, 1, 1) + mm(two, up, 1, 1)).astype(BF)


def feed_grads_body(mine, theirs, back_mine, back_theirs, *refs):
    gate_mine, gate_theirs, up_mine, up_theirs, inner_mine, inner_theirs, weights, out, own = refs
    for place, (left, right, mine_right, theirs_right) in enumerate(
        (
            (mine, theirs, gate_mine, gate_theirs),
            (mine, theirs, up_mine, up_theirs),
            (back_mine, back_theirs, inner_mine, inner_theirs),
        )
    ):
        part = mm(left[...], mine_right[...], 0, 0) + mm(right[...], theirs_right[...], 0, 0)
        out[:, place * DV : (place + 1) * DV] = part.astype(BF)
    own[...] = mm(gate_mine[...], weights[:, :DV], 1, 1) + mm(up_mine[...], weights[:, DV:], 1, 1)


def feed_grads(lefts, rights, weights):
    part, model = lefts[0].shape
    rows = 512
    halves = [
        pl.BlockSpec((part, DV), lambda i, half=half: (half, 0)) for _ in rights for half in range(2)
    ]
    return pl.pallas_call(
        feed_grads_body,
        grid=(model // rows,),
        out_shape=[pltpu.HBM((model, 3 * DV), BF), near(F32, part, model)],
        in_specs=[pl.BlockSpec((part, rows), lambda i: (0, i)) for _ in lefts]
        + halves
        + [pl.BlockSpec((rows, 2 * DV), lambda i: (i, 0))],
        out_specs=[
            pl.BlockSpec((rows, 3 * DV), lambda i: (i, 0)),
            pl.BlockSpec((part, rows), lambda i: (0, i)),
        ],
        compiler_params=pltpu.CompilerParams(vmem_limit_bytes=24 * 2**20),
        cost_estimate=pl.CostEstimate(
            flops=16 * part * model * DV, bytes_accessed=12 * model * DV, transcendentals=0
        ),
    )(*lefts, *[right for right in rights for _ in range(2)], weights)


def feed_out_body(inner, weight, own, other):
    size = own.shape[0]
    own[...] = mm(inner[:size, :], weight[...], 1, 1)
    other[...] = mm(inner[size:, :], weight[...], 1, 1).astype(BF)


def feed_out_shares(inner, weights):
    size, model = inner.shape[0] // 2, weights.shape[0]
    return pl.pallas_call(
        feed_out_body,
        grid=(model // DV,),
        out_shape=[shaped(F32, size, model), shaped(BF, size, 2 * model)],
        in_specs=[
            pl.BlockSpec(inner.shape, lambda i: (0, 0)),
            pl.BlockSpec((DV, DV), lambda i: (i, 2)),
        ],
        out_specs=[
            pl.BlockSpec((size, DV), lambda i: (0, i)),
            pl.BlockSpec((size, DV), lambda i: (0, i + model // DV)),
        ],
        compiler_params=pltpu.CompilerParams(vmem_limit_bytes=16 * 2**20),
        cost_estimate=pl.CostEstimate(
            flops=4 * size * model * DV, bytes_accessed=10 * size * model, transcendentals=0
        ),
    )(inner, pltpu.with_memory_space_constraint(weights, pltpu.HBM))


def last_share_body(qk, value, swish, qk_w, value_w, swish_w, kept, own, other):
    share = mm(qk[...], qk_w[...], 1, 1) + mm(value[...], value_w[...], 1, 1)
    share = share + mm(swish[...], swish_w[...], 1, 1)
    size = own.shape[0]
    own[...] = share[:size]
    other[...] = share[size:].astype(BF)


def last_share(rights, weights, joint):
    count, model = rights[0].shape[0], weights.shape[0]
    size = count // 2
    fixed = pl.BlockSpec((count, DV), lambda i: (0, 0))
    return pl.pallas_call(
        last_share_body,
        grid=(model // DV,),
        out_shape=[shaped(F32, size, model), shaped(BF, size, 2 * model)],
        in_specs=[fixed] * 3
        + [pl.BlockSpec((DV, DV), lambda i, j=j: (i, j)) for j in range(3)]
        + [pl.BlockSpec(memory_space=pl.ANY)],
        out_specs=[pl.BlockSpec((size, DV), lambda i: (0, i))] * 2,
        input_output_aliases={6: 1},
        compiler_params=pltpu.CompilerParams(vmem_limit_bytes=16 * 2**20),
        cost_estimate=pl.CostEstimate(
            flops=6 * count * model * DV, bytes_accessed=14 * count * model, transcendentals=0
        ),
    )(*rights, *[pltpu.with_memory_space_constraint(weights, pltpu.HBM)] * 3, joint)


def pair_body(z_ref, *refs):
    owns, received, outs = refs[: -SIDE - 1], refs[-SIDE - 1], refs[-SIDE:]
    height = outs[0].shape[0]
    for step, out in enumerate(outs):
        rows = slice(step * height, (step + 1) * height)
        column = 0
        for ref in owns:
            columns = slice(column, column + ref.shape[1])
            out[:, columns] = (ref[rows, :] + received[rows, columns].astype(F32)).astype(out.dtype)
            column += ref.shape[1]


def reduce_line(values, axis, dim, where):
    here = where[axis]
    total = block(values, here, dim)
    for step in (1, 2, 3):
        total = total + hop(block(values, here - step, dim), axis, step)
    return total


def local(
    tokens,
    mixer_gain,
    mixer_bias,
    query_weight,
    key_weight,
    value_weight,
    swish_weight,
    output_weight,
    feed_gain,
    feed_bias,
    gate_weight,
    up_weight,
    down_weight,
    cotangent,
):
    place = lax.axis_index("seq")
    where = {"y": place // 16, "x": place // 4 % 4, "z": place % 4}
    z, t = where["z"], lax.axis_index("tp")
    rows = tokens.shape[0]
    half = rows // 2
    shard = query_weight.shape[0]
    planes = [[16 * b + 4 * a + c for b in range(4) for a in range(4)] for c in range(4)]

    def own(values):
        return lax.dynamic_slice_in_dim(values, t * half, half, 0)

    pieces = pack(
        z,
        [
            query_weight,
            key_weight,
            value_weight,
            swish_weight,
            output_weight,
            gate_weight,
            up_weight,
            down_weight,
        ],
    )

    def gathered(parts):
        moved = [parts[0]] + [hop(parts[step], "z", step) for step in (1, 2, 3)]
        (share,) = whole(
            assemble_body, [jax.ShapeDtypeStruct((rows, parts[0].shape[1]), BF)], z, *moved
        )
        return share

    mixer_share = gathered(pieces[:SIDE])
    mixer_full = lax.all_gather(mixer_share, "seq", axis_index_groups=planes, axis=0, tiled=True)
    feed_share = gathered(pieces[SIDE:])
    tokens_own, upstream_own = own(tokens), own(cotangent)
    model = tokens.shape[1]
    both_mine, both_theirs, _ = gather_rows(jnp.concatenate([tokens_own, upstream_own], axis=1))
    upstream_mine, upstream_theirs = both_mine[:, model:], both_theirs[:, model:]
    normed = norm_rows(both_mine, both_theirs, mixer_gain, mixer_bias)
    normed_turned = turned(normed)

    number = jnp.arange(SIDE * rows)
    local_place = (
        ((z + number // half % SIDE) % SIDE) * rows
        + ((t + number // (SIDE * half)) % 2) * half
        + number % half
    )
    count = SIDE * rows
    positions = ((place // SIDE) * count + local_place).astype(F32)
    frequency = 1.0 / 10000.0 ** jnp.linspace(0.0, 1.0, DK // 2, dtype=F32)
    phases = positions[:, None] * frequency[None, :]
    cosine, sine = jnp.cos(phases), jnp.sin(phases)

    def turn(values):
        a, b = values[:, : DK // 2], values[:, DK // 2 :]
        return jnp.concatenate([a * cosine - b * sine, b * cosine + a * sine], axis=1)

    def turn_back(values):
        a, b = values[:, : DK // 2], values[:, DK // 2 :]
        return jnp.concatenate([a * cosine + b * sine, b * cosine - a * sine], axis=1)

    rate = jnp.log(1.0 - 2.0 ** (-5.0 - (SIDE * t + z).astype(F32)))
    places = local_place.astype(F32)
    offsets = places[:, None] - places[None, :]
    within = jnp.where(offsets >= 0, jnp.exp(jnp.maximum(offsets, 0.0) * rate), 0.0)
    onward = jnp.exp(places * rate)[:, None]
    leftover = jnp.exp((count - places) * rate)[:, None]

    weights = [scan_weights(count, rate, where, backward) for backward in (False, True)]
    early = (
        feed_share,
        normed,
        normed_turned,
        upstream_mine,
        upstream_theirs,
        cosine,
        sine,
        within,
        leftover,
        onward,
        weights,
    )
    (
        feed_share,
        normed,
        normed_turned,
        upstream_mine,
        upstream_theirs,
        cosine,
        sine,
        within,
        leftover,
        onward,
        weights,
    ) = lax.optimization_barrier(early)
    feed_full = lax.all_gather(feed_share, "seq", axis_index_groups=planes, axis=0, tiled=True)
    query, key, value, key_left = project(normed, mixer_full, cosine, sine, leftover)
    mixer_rest, value = lax.optimization_barrier((mixer_full, value))
    sw_full, out_full = lax.optimization_barrier(
        (mixer_rest[:, 2 * DV : 3 * DV], mixer_rest[:, 3 * DV :])
    )
    incoming, switch = scan(key_left, value, weights[0], where, mm(normed, sw_full))
    scores = (mm(query, key, 1, 1) * within).astype(BF)
    retained = mm(scores, value) + mm(query, incoming) * onward
    normal_ret, scale_ret = layer_stats(retained)
    swish_act = jax.nn.silu(switch)
    branch = (swish_act * normal_ret).astype(BF)
    part = branch.shape[0] // 2
    shares_one = ring_shares(
        mm(branch[:part], out_full, 1, 1), mm(branch[part:], out_full, 1, 1), z
    )
    grad_inner = whole(
        feed_back_body,
        [shaped(F32, part, DV)] * 2,
        z,
        upstream_mine,
        upstream_theirs,
        feed_full,
        flops=4 * part * upstream_mine.shape[1] * DV,
    )
    attended = total_of(shares_one)

    residual_in = tokens_own.astype(F32)
    residual = residual_in + attended
    normal_two, scale_two = layer_stats(residual)
    *normed_two, grad_inner = gather_rows(
        (normal_two * feed_gain + feed_bias).astype(BF), grad_inner
    )
    inner_act, grad_gate, grad_up, other_share = whole(
        feed_body,
        [near(BF, count, DV)] * 3 + [near(BF, part, model)],
        z,
        *normed_two,
        *grad_inner,
        feed_full,
        flops=16 * part * model * DV,
    )
    feed_terms, own_share = feed_grads(
        [*normed_two, upstream_mine, upstream_theirs], [grad_gate, grad_up, inner_act], feed_full
    )
    feed_sum = lax.psum_scatter(
        feed_terms, "seq", axis_index_groups=planes, scatter_dimension=0, tiled=True
    )
    received = swap(other_share)
    received, feed_terms = lax.optimization_barrier((received, feed_terms))
    pair_two = whole(
        pair_body,
        [shaped(F32, half, model)] + [shaped(BF, half, model)] * 3,
        z,
        own_share,
        received,
    )
    shares_two = [pair_two[0]] + [hop(pair_two[step], "z", -step) for step in (1, 2, 3)]
    grad_norm_two = total_of(shares_two)
    upstream = upstream_own.astype(F32)
    grad_resid = upstream + norm_back(grad_norm_two * feed_gain, normal_two, scale_two)
    *grad_attended, _ = gather_rows(grad_resid.astype(BF))

    grad_branch = jnp.concatenate([mm(rows_half, out_full) for rows_half in grad_attended], axis=0)
    grad_switch = (grad_branch * normal_ret * silu_slope(switch)).astype(BF)
    grad_low = norm_back(grad_branch * swish_act, normal_ret, scale_ret).astype(BF)
    grad_onward = (grad_low.astype(F32) * onward).astype(BF)
    early_terms = grads(
        [[(0, 0)], [(1, 1), (2, 2)]],
        [normed_turned, *grad_attended],
        [0],
        [grad_switch, branch[:part], branch[part:]],
        2,
        0,
    )
    outgoing, _ = scan(query, grad_onward, weights[1], where, None)
    grad_scores = (mm(grad_low, value, 1, 1) * within).astype(BF)
    grad_query = mm(grad_scores, key) + mm(grad_onward, incoming, 1, 1)
    grad_key = mm(grad_scores, query, 0, 0) + mm(value, outgoing, 1, 1) * leftover
    grad_value = mm(scores, grad_low, 0, 0) + mm(key_left, outgoing)
    query_grads = turn_back(grad_query).astype(BF)
    key_grads = (turn_back(grad_key) * DK ** (-0.5)).astype(BF)
    qk_grads = jnp.concatenate([query_grads, key_grads], axis=1)
    value_grads = grad_value.astype(BF)

    mixer_terms = grads(
        [[(0, 0)], [(0, 1)]], [normed_turned], [0], [qk_grads, value_grads], 2, 1, early_terms
    )
    mixer_terms, feed_sum = lax.optimization_barrier((mixer_terms, feed_sum))
    mixer_sum = lax.psum_scatter(
        mixer_terms, "seq", axis_index_groups=planes, scatter_dimension=0, tiled=True
    )

    mixer_terms, qk_grads, value_grads, grad_switch, inner_act = lax.optimization_barrier(
        (mixer_terms, qk_grads, value_grads, grad_switch, inner_act)
    )
    feed_own, joint = feed_out_shares(inner_act, feed_full)
    share_own, joint = last_share([qk_grads, value_grads, grad_switch], mixer_full, joint)
    joint_pair = whole(
        pair_body,
        [shaped(F32, half, 2 * model)] + [shaped(BF, half, 2 * model)] * 3,
        z,
        share_own,
        feed_own,
        swap(joint),
    )
    joint_total = total_of(
        [joint_pair[0]] + [hop(joint_pair[step], "z", -step) for step in (1, 2, 3)]
    )
    grad_norm_one = joint_total[:, :model]
    block_output = (residual + joint_total[:, model:]).astype(BF)
    normal_own, scale_own = layer_stats(residual_in)
    tokens_grad = grad_resid + norm_back(grad_norm_one * mixer_gain, normal_own, scale_own)
    norms = jnp.stack(
        [
            jnp.sum(grad_norm_one * normal_own, axis=0),
            jnp.sum(grad_norm_one, axis=0),
            jnp.sum(grad_norm_two * normal_two, axis=0),
            jnp.sum(grad_norm_two, axis=0),
        ]
    )
    norms = norms.reshape(4, SIDE, SIDE, SIDE, -1).transpose(1, 2, 3, 0, 4)
    norms = norms.reshape(SIDE, SIDE, SIDE, -1)
    for axis, dim in (("x", 1), ("y", 0), ("z", 0)):
        norms = reduce_line(norms, axis, dim, where)
    norms = norms.reshape(1, -1)
    norms = (norms + swap(norms)).reshape(4, -1)

    def cut_rows(summed):
        return whole(cut_body, [shaped(BF, shard, summed.shape[1])] * SIDE, z, summed)

    def returned(parts, widths, paired):
        moved = [parts[0]] + [hop(parts[step], "z", step) for step in (1, 2, 3)]
        outs = [shaped(F32, shard, SIDE * width) for width in widths]
        return whole(lambda *refs: unpack_body(paired, *refs), outs, z, *moved)

    gate_sum, up_sum, down_sum = returned(cut_rows(feed_sum), [DV] * 3, ())
    swish_sum, output_sum, query_sum, key_sum, value_sum = returned(
        cut_rows(mixer_sum), [DV, DV, DK, DK, DV], (2, 3)
    )

    def both_halves(values):
        theirs = swap(values)
        return jnp.concatenate(
            [jnp.where(t == 0, values, theirs), jnp.where(t == 0, theirs, values)], axis=0
        )

    return (
        both_halves(block_output),
        both_halves(tokens_grad),
        norms[0],
        norms[1],
        query_sum,
        key_sum,
        value_sum,
        swish_sum,
        output_sum,
        norms[2],
        norms[3],
        gate_sum,
        up_sum,
        down_sum,
    )


def solution(mesh):
    split = P("seq", "tp")
    token = P("seq", None)
    in_specs = (token, P(), P()) + (split,) * 5 + (P(), P()) + (split,) * 3 + (token,)
    out_specs = (token, token, P("seq"), P("seq")) + (split,) * 5 + (P("seq"), P("seq")) + (split,) * 3
    return jax.shard_map(local, mesh=mesh, in_specs=in_specs, out_specs=out_specs, check_vma=False)
```

```python
import jax
import jax.numpy as jnp
from jax import lax
from jax.experimental import pallas as pl
from jax.experimental.pallas import tpu as pltpu
from jax.sharding import PartitionSpec as P

DK = 256
DV = 512
SIDE = 4
BF = jnp.bfloat16
F32 = jnp.float32
STRIDE = {"y": 16, "x": 4, "z": 1}


def pairs(axis, step):
    table = []
    for source in range(64):
        place = source // STRIDE[axis] % SIDE
        target = source + ((place - step) % SIDE - place) * STRIDE[axis]
        table.append((source, target))
    return table


def hop(value, axis, step):
    return lax.ppermute(value, "seq", pairs(axis, step % SIDE))


def swap(value):
    return lax.ppermute(value, "tp", [(0, 1), (1, 0)])


def direct(value, axis):
    return [value] + [hop(value, axis, step) for step in (1, 2, 3)]


def block(values, index, axis=0):
    return lax.dynamic_index_in_dim(values, index % SIDE, axis, keepdims=False)


def gather_rows(rows, beside=None):
    parts = direct(rows, "z")
    if beside is not None:
        parts[1], beside = lax.optimization_barrier((parts[1], beside))
    mine = jnp.concatenate(parts, axis=0)
    return (mine, swap(mine), beside)


def ring_shares(own, other, z):
    height, model = own.shape[0] // SIDE, own.shape[1]
    pair = whole(
        pair_body,
        [shaped(F32, height, model)] + [shaped(BF, height, model)] * 3,
        z,
        own,
        swap(other.astype(BF)),
    )
    return [pair[0]] + [hop(pair[step], "z", -step) for step in (1, 2, 3)]


def total_of(shares):
    return sum(share.astype(F32) for share in shares[1:]) + shares[0]


def whole(body, outs, scalars, *arrays, flops=0):
    vmem = pl.BlockSpec(memory_space=pltpu.VMEM)
    moved = sum(array.size * array.dtype.itemsize for array in arrays)
    if scalars.ndim == 0:
        scalars = scalars.reshape(1).astype(jnp.int32)
    return pl.pallas_call(
        body,
        out_shape=outs,
        in_specs=[pl.BlockSpec(memory_space=pltpu.SMEM)] + [vmem] * len(arrays),
        out_specs=[vmem] * len(outs),
        compiler_params=pltpu.CompilerParams(vmem_limit_bytes=16 * 2**20),
        cost_estimate=pl.CostEstimate(flops=flops, bytes_accessed=moved, transcendentals=0),
    )(scalars, *arrays)


def near(dtype, *shape):
    return pltpu.VMEM(shape, dtype)


def shaped(dtype, *shape):
    return jax.ShapeDtypeStruct(shape, dtype)


def head_of(z_ref, step):
    return lax.rem(z_ref[0] + SIDE + step, SIDE)


def lanes(ref, head, width):
    return ref[:, pl.ds(pl.multiple_of(head * width, width), width)]


def pack_body(z_ref, *refs):
    sources, pieces = refs[:8], refs[8 : 8 + 2 * SIDE]
    held, sems = refs[8 + 2 * SIDE : -1], refs[-1]
    copies = [
        pltpu.make_async_copy(source, ref, sems.at[place])
        for place, (source, ref) in enumerate(zip(sources, held))
    ]
    for copy in copies:
        copy.start()
    old = lax.broadcasted_iota(jnp.int32, (DK, DK), 0)
    new = lax.broadcasted_iota(jnp.int32, (DK, DK), 1)
    shuffle = (old == jnp.where(new < DK // 2, 2 * new, 2 * new - DK + 1)).astype(F32).astype(BF)
    for place, ref in enumerate(held):
        copies[place].wait()
        for step in range(SIDE):
            head = head_of(z_ref, -step)
            if place < 2:
                part = jnp.dot(lanes(ref, head, DK), shuffle, preferred_element_type=F32)
                pieces[step][:, place * DK : (place + 1) * DK] = part.astype(BF)
            elif place < 5:
                pieces[step][:, (place - 1) * DV : place * DV] = lanes(ref, head, DV)
            else:
                pieces[SIDE + step][:, (place - 5) * DV : (place - 4) * DV] = lanes(ref, head, DV)


def pack(z, weights):
    vmem = pl.BlockSpec(memory_space=pltpu.VMEM)
    shard = weights[0].shape[0]
    outs = [jax.ShapeDtypeStruct((shard, 2 * DK + 3 * DV), BF)] * SIDE
    outs = outs + [jax.ShapeDtypeStruct((shard, 3 * DV), BF)] * SIDE
    return pl.pallas_call(
        pack_body,
        out_shape=outs,
        in_specs=[pl.BlockSpec(memory_space=pltpu.SMEM)]
        + [pl.BlockSpec(memory_space=pl.ANY)] * len(weights),
        out_specs=[vmem] * len(outs),
        scratch_shapes=[pltpu.VMEM(weight.shape, BF) for weight in weights]
        + [pltpu.SemaphoreType.DMA((len(weights),))],
        compiler_params=pltpu.CompilerParams(vmem_limit_bytes=16 * 2**20),
    )(
        z.reshape(1).astype(jnp.int32),
        *[pltpu.with_memory_space_constraint(weight, pltpu.HBM) for weight in weights],
    )


def cut_body(z_ref, whole_ref, *pieces):
    height = pieces[0].shape[0]
    for step, piece in enumerate(pieces):
        row = pl.multiple_of(head_of(z_ref, -step) * height, height)
        piece[...] = whole_ref[pl.ds(row, height), :]


def unpack_body(paired, z_ref, *refs):
    outs = refs[SIDE:]
    old = lax.broadcasted_iota(jnp.int32, (DK, DK), 1)
    new = lax.broadcasted_iota(jnp.int32, (DK, DK), 0)
    shuffle = (old == jnp.where(new < DK // 2, 2 * new, 2 * new - DK + 1)).astype(F32).astype(BF)
    for step in range(SIDE):
        piece = refs[step]
        head = head_of(z_ref, step)
        start = 0
        for place, out in enumerate(outs):
            width = out.shape[1] // SIDE
            part = piece[:, start : start + width]
            if place in paired:
                part = jnp.dot(part, shuffle, preferred_element_type=F32)
            out[:, pl.ds(pl.multiple_of(head * width, width), width)] = part.astype(F32)
            start += width


def assemble_body(z_ref, *refs):
    for step in range(SIDE):
        piece = refs[step]
        height = piece.shape[0]
        row = pl.multiple_of(head_of(z_ref, step) * height, height)
        column = 0
        for whole_ref in refs[SIDE:]:
            width = whole_ref.shape[1]
            whole_ref[pl.ds(row, height), :] = piece[:, column : column + width]
            column += width


def grads_body(terms, turned, lefts, *refs):
    left, right, out = refs[:lefts], refs[lefts : lefts + terms[-1][-1][1] + 1], refs[-1]
    for place, term in enumerate(terms):
        part = 0.0
        for a, b in term:
            part = part + mm(left[a][...], right[b][...], int(a in turned), 0)
        out[:, place * DV : (place + 1) * DV] = part.astype(BF)


def grads(terms, lefts, turned, rights, groups=1, group=0, into=None, rows=512):
    model = lefts[0].shape[0 if 0 in turned else 1]
    specs = [
        pl.BlockSpec((rows, left.shape[1]), lambda i: (i, 0))
        if place in turned
        else pl.BlockSpec((left.shape[0], rows), lambda i: (0, i))
        for place, left in enumerate(lefts)
    ]
    specs = specs + [pl.BlockSpec(right.shape, lambda i: (0, 0)) for right in rights]
    arrays = [*lefts, *rights]
    if into is not None:
        specs.append(pl.BlockSpec(memory_space=pl.ANY))
        arrays.append(into)
    width = len(terms) * DV
    return pl.pallas_call(
        lambda *refs: grads_body(terms, turned, len(lefts), *refs),
        grid=(model // rows,),
        out_shape=pltpu.HBM((model, groups * width), BF),
        in_specs=specs,
        out_specs=pl.BlockSpec((rows, width), lambda i: (i, group)),
        input_output_aliases={} if into is None else {len(arrays) - 1: 0},
        compiler_params=pltpu.CompilerParams(vmem_limit_bytes=20 * 2**20),
        cost_estimate=pl.CostEstimate(
            flops=2 * 512 * model * width, bytes_accessed=2 * model * (width + 512), transcendentals=0
        ),
    )(*arrays)


def norm_body(mine, theirs, gain, bias, out):
    def run(ref):
        values = ref[...].astype(F32)
        centred = values - jnp.mean(values, axis=-1, keepdims=True)
        scaling = lax.rsqrt(jnp.mean(centred * centred, axis=-1, keepdims=True) + 1e-05)
        out[...] = (centred * scaling * gain[...] + bias[...]).astype(BF)

    pl.when(pl.program_id(0) < SIDE)(lambda: run(mine))
    pl.when(pl.program_id(0) >= SIDE)(lambda: run(theirs))


def norm_rows(mine, theirs, gain, bias):
    size, model = mine.shape[0], gain.shape[0]
    part = size // SIDE
    vector = pl.BlockSpec((1, model), lambda i: (0, 0))
    return pl.pallas_call(
        norm_body,
        grid=(2 * SIDE,),
        out_shape=shaped(BF, 2 * size, model),
        in_specs=[
            pl.BlockSpec((part, model), lambda i: (jnp.minimum(i, SIDE - 1), 0)),
            pl.BlockSpec((part, model), lambda i: (jnp.maximum(i - SIDE, 0), 0)),
            vector,
            vector,
        ],
        out_specs=pl.BlockSpec((part, model), lambda i: (i, 0)),
        cost_estimate=pl.CostEstimate(
            flops=20 * size * model, bytes_accessed=12 * size * model, transcendentals=0
        ),
    )(mine, theirs, gain.reshape(1, -1), bias.reshape(1, -1))


def turn_body(rows, out):
    out[...] = rows[...].T


def turned(rows):
    size, model = rows.shape
    return pl.pallas_call(
        turn_body,
        grid=(model // size,),
        out_shape=shaped(rows.dtype, model, size),
        in_specs=[pl.BlockSpec((size, size), lambda i: (0, i))],
        out_specs=pl.BlockSpec((size, size), lambda i: (i, 0)),
        cost_estimate=pl.CostEstimate(
            flops=size * model, bytes_accessed=4 * size * model, transcendentals=0
        ),
    )(rows)


def state_body(x_ref, left, right, *pieces):
    for step, piece in enumerate(pieces):
        width = piece.shape[1]
        part = lax.dot_general(
            left[...],
            lanes(right, head_of(x_ref, -step), width),
            (((0,), (0,)), ((), ())),
            preferred_element_type=F32,
        )
        piece[...] = part.astype(piece.dtype)


def mix_body(weights, *refs):
    count = weights.shape[1]
    for place, out in enumerate(refs[count:]):
        total = 0.0
        for source in range(count):
            total = total + weights[place, source] * refs[source][...].astype(F32)
        out[...] = total.astype(out.dtype)


def quarters_body(x_ref, *refs):
    out = refs[-1]
    for step, piece in enumerate(refs[:-1]):
        width = piece.shape[1]
        start = pl.multiple_of(head_of(x_ref, step) * width, width)
        out[:, pl.ds(start, width)] = piece[...].astype(out.dtype)


def layer_stats(values):
    centred = values - jnp.mean(values, axis=-1, keepdims=True)
    scaling = lax.rsqrt(jnp.mean(centred * centred, axis=-1, keepdims=True) + 1e-05)
    return (centred * scaling, scaling)


def norm_back(grad_hat, normal, scaling):
    return scaling * (
        grad_hat
        - jnp.mean(grad_hat, axis=-1, keepdims=True)
        - normal * jnp.mean(grad_hat * normal, axis=-1, keepdims=True)
    )


def silu_slope(values):
    logistic = jax.nn.sigmoid(values)
    return logistic * (1.0 + values * (1.0 - logistic))


def mm(left, right, left_dim=1, right_dim=0):
    return lax.dot_general(
        left, right, (((left_dim,), (right_dim,)), ((), ())), preferred_element_type=F32
    )


def scan_weights(size, rate, where, backward):
    x, y = where["x"], where["y"]
    steps = jnp.arange(SIDE)

    def mirrored(index):
        return SIDE - 1 - index % SIDE if backward else index % SIDE

    def power(count):
        return jnp.exp(count.astype(F32) * size * rate)

    sources, targets = mirrored(x + steps), mirrored(x - steps)
    lines, line = mirrored(y + steps), mirrored(y)
    to_line = power(SIDE - 1 - sources)
    from_line = jnp.where(lines < line, power(SIDE * jnp.maximum(line - 1 - lines, 0)), 0.0)
    gap = targets[:, None] - 1 - sources[None, :]
    within = jnp.where(gap >= 0, power(jnp.maximum(gap, 0)), 0.0)
    reach = power(targets)[:, None] * from_line[None, 1:]
    return to_line[None, :], jnp.concatenate([within, reach], axis=1)


def scan(left, right, weights, where, beside):
    x = where["x"]
    shape = (left.shape[1], right.shape[1] // SIDE)
    pieces = whole(state_body, [shaped(F32, *shape)] + [shaped(BF, *shape)] * 3, x, left, right)
    got = [pieces[0]] + [hop(pieces[step], "x", step) for step in (1, 2, 3)]
    (total,) = whole(mix_body, [shaped(BF, *shape)], weights[0], *got)
    others = [hop(total, "y", step) for step in (1, 2, 3)]
    given = whole(mix_body, [shaped(BF, *shape)] * SIDE, weights[1], *got, *others)
    moved = [given[0]] + [hop(given[step], "x", step) for step in (1, 2, 3)]
    if beside is not None:
        moved[1], beside = lax.optimization_barrier((moved[1], beside))
    (joined,) = whole(quarters_body, [near(BF, shape[0], right.shape[1])], x, *moved)
    return joined, beside


def project_body(rows_in, weight_in, *refs):
    tables_in, (query, key, value, key_left) = refs[:3], refs[3:7]
    rows, weight, *tables, sems = refs[7:]
    width = weight.shape[1]
    depth = weight.shape[0] // SIDE
    copies = []
    for step in range(SIDE):
        part = pl.ds(step * depth, depth)
        source = weight_in.at[part, pl.ds(0, width)]
        copies.append(pltpu.make_async_copy(source, weight.at[part], sems.at[2 * step]))
        source = rows_in.at[:, part]
        copies.append(pltpu.make_async_copy(source, rows.at[:, part], sems.at[2 * step + 1]))
    for place, (source, table) in enumerate(zip(tables_in, tables)):
        copies.append(pltpu.make_async_copy(source, table, sems.at[2 * SIDE + place]))
    for copy in copies:
        copy.start()
    total = 0.0
    for step in range(SIDE):
        copies[2 * step].wait()
        copies[2 * step + 1].wait()
        part = slice(step * depth, (step + 1) * depth)
        total = total + jnp.dot(rows[:, part], weight[part, :], preferred_element_type=F32)
    for copy in copies[2 * SIDE :]:
        copy.wait()
    cosine, sine, left_over = tables
    half = DK // 2
    for place in range(2):
        a = total[:, place * DK : place * DK + half]
        b = total[:, place * DK + half : (place + 1) * DK]
        turned_halves = (a * cosine[...] - b * sine[...], b * cosine[...] + a * sine[...])
        for index, turned_half in enumerate(turned_halves):
            columns = slice(index * half, (index + 1) * half)
            if place == 0:
                query[:, columns] = turned_half.astype(BF)
            else:
                key[:, columns] = (turned_half * DK ** (-0.5)).astype(BF)
                key_left[:, columns] = (key[:, columns].astype(F32) * left_over[...]).astype(BF)
    value[...] = total[:, 2 * DK :].astype(BF)


def project(rows, weight, cosine, sine, leftover):
    size, model = rows.shape
    vmem = pl.BlockSpec(memory_space=pltpu.VMEM)
    kept = pl.BlockSpec(memory_space=pl.ANY)
    steps = 2 + DV // DK
    return pl.pallas_call(
        project_body,
        out_shape=[
            near(BF, size, DK),
            near(BF, size, DK),
            near(BF, size, DV),
            near(BF, size, DK),
        ],
        in_specs=[kept] * 5,
        out_specs=[vmem] * 4,
        scratch_shapes=[
            pltpu.VMEM((size, model), BF),
            pltpu.VMEM((model, steps * DK), BF),
            *[pltpu.VMEM(table.shape, F32) for table in (cosine, sine, leftover)],
            pltpu.SemaphoreType.DMA((2 * SIDE + 3,)),
        ],
        compiler_params=pltpu.CompilerParams(vmem_limit_bytes=20 * 2**20),
        cost_estimate=pl.CostEstimate(
            flops=2 * size * model * steps * DK, bytes_accessed=2 * model * steps * DK, transcendentals=0
        ),
    )(
        *[
            pltpu.with_memory_space_constraint(array, pltpu.HBM)
            for array in (rows, weight, cosine, sine, leftover)
        ]
    )


def feed_back_body(z_ref, first, second, weights, *outs):
    for rows, out in zip((first, second), outs):
        out[...] = jnp.dot(rows[...], weights[:, 2 * DV :], preferred_element_type=F32)


def feed_body(z_ref, mine, theirs, back_mine, back_theirs, weights, *outs):
    inner, grad_gate, grad_up, share = outs
    gate, up = weights[:, :DV], weights[:, DV : 2 * DV]
    size = mine.shape[0]
    for place, (rows, grad_inner) in enumerate(((theirs, back_theirs), (mine, back_mine))):
        gate_pre = jnp.dot(rows[...], gate, preferred_element_type=F32)
        upward = jnp.dot(rows[...], up, preferred_element_type=F32)
        logistic = jax.nn.sigmoid(gate_pre)
        gate_act = gate_pre * logistic
        slope = logistic * (1.0 + gate_pre * (1.0 - logistic))
        one = (grad_inner[...] * upward * slope).astype(BF)
        two = (grad_inner[...] * gate_act).astype(BF)
        kept = slice((1 - place) * size, (2 - place) * size)
        inner[kept, :] = (gate_act * upward).astype(BF)
        grad_gate[kept, :] = one
        grad_up[kept, :] = two
        if place == 0:
            share[...] = (mm(one, gate, 1, 1) + mm(two, up, 1, 1)).astype(BF)


def feed_pair_body(grad_gate, grad_up, weights, received, *outs):
    height = outs[0].shape[0]
    own = mm(grad_gate[...], weights[:, :DV], 1, 1) + mm(grad_up[...], weights[:, DV:], 1, 1)
    for step, out in enumerate(outs):
        rows = slice(step * height, (step + 1) * height)
        out[...] = (own[rows] + received[rows, :].astype(F32)).astype(out.dtype)


def feed_pair(grad_gate, grad_up, weights, received):
    size, model = received.shape
    half = pl.BlockSpec((size, DV), lambda i: (0, 0))
    columns = lambda height: pl.BlockSpec((height, DV), lambda i: (0, i))
    return pl.pallas_call(
        feed_pair_body,
        grid=(model // DV,),
        out_shape=[shaped(F32 if step == 0 else BF, size // SIDE, model) for step in range(SIDE)],
        in_specs=[half, half, pl.BlockSpec((DV, 2 * DV), lambda i: (i, 0)), columns(size)],
        out_specs=[columns(size // SIDE)] * SIDE,
        compiler_params=pltpu.CompilerParams(vmem_limit_bytes=16 * 2**20),
        cost_estimate=pl.CostEstimate(
            flops=4 * size * model * DV, bytes_accessed=8 * model * DV, transcendentals=0
        ),
    )(grad_gate, grad_up, pltpu.with_memory_space_constraint(weights, pltpu.HBM), received)


def feed_out_body(inner, weight, own, other):
    size = own.shape[0]
    own[...] = mm(inner[:size, :], weight[...], 1, 1)
    other[...] = mm(inner[size:, :], weight[...], 1, 1).astype(BF)


def feed_out_shares(inner, weights):
    size, model = inner.shape[0] // 2, weights.shape[0]
    return pl.pallas_call(
        feed_out_body,
        grid=(model // DV,),
        out_shape=[shaped(F32, size, model), shaped(BF, size, 2 * model)],
        in_specs=[
            pl.BlockSpec(inner.shape, lambda i: (0, 0)),
            pl.BlockSpec((DV, DV), lambda i: (i, 2)),
        ],
        out_specs=[
            pl.BlockSpec((size, DV), lambda i: (0, i)),
            pl.BlockSpec((size, DV), lambda i: (0, i + model // DV)),
        ],
        compiler_params=pltpu.CompilerParams(vmem_limit_bytes=16 * 2**20),
        cost_estimate=pl.CostEstimate(
            flops=4 * size * model * DV, bytes_accessed=10 * size * model, transcendentals=0
        ),
    )(inner, pltpu.with_memory_space_constraint(weights, pltpu.HBM))


def last_share_body(qk, value, swish, qk_w, value_w, swish_w, kept, own, other):
    share = mm(qk[...], qk_w[...], 1, 1) + mm(value[...], value_w[...], 1, 1)
    share = share + mm(swish[...], swish_w[...], 1, 1)
    size = own.shape[0]
    own[...] = share[:size]
    other[...] = share[size:].astype(BF)


def last_share(rights, weights, joint):
    count, model = rights[0].shape[0], weights.shape[0]
    size = count // 2
    fixed = pl.BlockSpec((count, DV), lambda i: (0, 0))
    return pl.pallas_call(
        last_share_body,
        grid=(model // DV,),
        out_shape=[shaped(F32, size, model), shaped(BF, size, 2 * model)],
        in_specs=[fixed] * 3
        + [pl.BlockSpec((DV, DV), lambda i, j=j: (i, j)) for j in range(3)]
        + [pl.BlockSpec(memory_space=pl.ANY)],
        out_specs=[pl.BlockSpec((size, DV), lambda i: (0, i))] * 2,
        input_output_aliases={6: 1},
        compiler_params=pltpu.CompilerParams(vmem_limit_bytes=16 * 2**20),
        cost_estimate=pl.CostEstimate(
            flops=6 * count * model * DV, bytes_accessed=14 * count * model, transcendentals=0
        ),
    )(*rights, *[pltpu.with_memory_space_constraint(weights, pltpu.HBM)] * 3, joint)


def pair_body(z_ref, *refs):
    owns, received, outs = refs[: -SIDE - 1], refs[-SIDE - 1], refs[-SIDE:]
    height = outs[0].shape[0]
    for step, out in enumerate(outs):
        rows = slice(step * height, (step + 1) * height)
        column = 0
        for ref in owns:
            columns = slice(column, column + ref.shape[1])
            out[:, columns] = (ref[rows, :] + received[rows, columns].astype(F32)).astype(out.dtype)
            column += ref.shape[1]


def reduce_line(values, axis, dim, where):
    here = where[axis]
    total = block(values, here, dim)
    for step in (1, 2, 3):
        total = total + hop(block(values, here - step, dim), axis, step)
    return total


def local(
    tokens,
    mixer_gain,
    mixer_bias,
    query_weight,
    key_weight,
    value_weight,
    swish_weight,
    output_weight,
    feed_gain,
    feed_bias,
    gate_weight,
    up_weight,
    down_weight,
    cotangent,
):
    place = lax.axis_index("seq")
    where = {"y": place // 16, "x": place // 4 % 4, "z": place % 4}
    z, t = where["z"], lax.axis_index("tp")
    rows = tokens.shape[0]
    half = rows // 2
    shard = query_weight.shape[0]
    planes = [[16 * b + 4 * a + c for b in range(4) for a in range(4)] for c in range(4)]

    def own(values):
        return lax.dynamic_slice_in_dim(values, t * half, half, 0)

    pieces = pack(
        z,
        [
            query_weight,
            key_weight,
            value_weight,
            swish_weight,
            output_weight,
            gate_weight,
            up_weight,
            down_weight,
        ],
    )

    def gathered(parts):
        moved = [parts[0]] + [hop(parts[step], "z", step) for step in (1, 2, 3)]
        (share,) = whole(
            assemble_body, [jax.ShapeDtypeStruct((rows, parts[0].shape[1]), BF)], z, *moved
        )
        return share

    mixer_share = gathered(pieces[:SIDE])
    mixer_full = lax.all_gather(mixer_share, "seq", axis_index_groups=planes, axis=0, tiled=True)
    feed_share = gathered(pieces[SIDE:])
    tokens_own, upstream_own = own(tokens), own(cotangent)
    model = tokens.shape[1]
    both_mine, both_theirs, _ = gather_rows(jnp.concatenate([tokens_own, upstream_own], axis=1))
    upstream_mine, upstream_theirs = both_mine[:, model:], both_theirs[:, model:]
    normed = norm_rows(both_mine, both_theirs, mixer_gain, mixer_bias)
    normed_turned = turned(normed)

    number = jnp.arange(SIDE * rows)
    local_place = (
        ((z + number // half % SIDE) % SIDE) * rows
        + ((t + number // (SIDE * half)) % 2) * half
        + number % half
    )
    count = SIDE * rows
    positions = ((place // SIDE) * count + local_place).astype(F32)
    frequency = 1.0 / 10000.0 ** jnp.linspace(0.0, 1.0, DK // 2, dtype=F32)
    phases = positions[:, None] * frequency[None, :]
    cosine, sine = jnp.cos(phases), jnp.sin(phases)

    def turn(values):
        a, b = values[:, : DK // 2], values[:, DK // 2 :]
        return jnp.concatenate([a * cosine - b * sine, b * cosine + a * sine], axis=1)

    def turn_back(values):
        a, b = values[:, : DK // 2], values[:, DK // 2 :]
        return jnp.concatenate([a * cosine + b * sine, b * cosine - a * sine], axis=1)

    rate = jnp.log(1.0 - 2.0 ** (-5.0 - (SIDE * t + z).astype(F32)))
    places = local_place.astype(F32)
    offsets = places[:, None] - places[None, :]
    within = jnp.where(offsets >= 0, jnp.exp(jnp.maximum(offsets, 0.0) * rate), 0.0)
    onward = jnp.exp(places * rate)[:, None]
    leftover = jnp.exp((count - places) * rate)[:, None]

    weights = [scan_weights(count, rate, where, backward) for backward in (False, True)]
    early = (
        feed_share,
        normed,
        normed_turned,
        upstream_mine,
        upstream_theirs,
        cosine,
        sine,
        within,
        leftover,
        onward,
        weights,
    )
    (
        feed_share,
        normed,
        normed_turned,
        upstream_mine,
        upstream_theirs,
        cosine,
        sine,
        within,
        leftover,
        onward,
        weights,
    ) = lax.optimization_barrier(early)
    feed_full = lax.all_gather(feed_share, "seq", axis_index_groups=planes, axis=0, tiled=True)
    query, key, value, key_left = project(normed, mixer_full, cosine, sine, leftover)
    mixer_rest, value = lax.optimization_barrier((mixer_full, value))
    sw_full, out_full = lax.optimization_barrier(
        (mixer_rest[:, 2 * DV : 3 * DV], mixer_rest[:, 3 * DV :])
    )
    incoming, switch = scan(key_left, value, weights[0], where, mm(normed, sw_full))
    scores = (mm(query, key, 1, 1) * within).astype(BF)
    retained = mm(scores, value) + mm(query, incoming) * onward
    normal_ret, scale_ret = layer_stats(retained)
    swish_act = jax.nn.silu(switch)
    branch = (swish_act * normal_ret).astype(BF)
    part = branch.shape[0] // 2
    shares_one = ring_shares(
        mm(branch[:part], out_full, 1, 1), mm(branch[part:], out_full, 1, 1), z
    )
    grad_inner = whole(
        feed_back_body,
        [shaped(F32, part, DV)] * 2,
        z,
        upstream_mine,
        upstream_theirs,
        feed_full,
        flops=4 * part * upstream_mine.shape[1] * DV,
    )
    attended = total_of(shares_one)

    residual_in = tokens_own.astype(F32)
    residual = residual_in + attended
    normal_two, scale_two = layer_stats(residual)
    *normed_two, grad_inner = gather_rows(
        (normal_two * feed_gain + feed_bias).astype(BF), grad_inner
    )
    inner_act, grad_gate, grad_up, other_share = whole(
        feed_body,
        [near(BF, count, DV)] * 3 + [near(BF, part, model)],
        z,
        *normed_two,
        *grad_inner,
        feed_full,
        flops=16 * part * model * DV,
    )
    halves = (slice(0, part), slice(part, count))
    feed_terms = grads(
        [[(0, 0), (1, 1)], [(0, 2), (1, 3)], [(2, 4), (3, 5)]],
        [*normed_two, upstream_mine, upstream_theirs],
        [],
        [array[rows_half] for array in (grad_gate, grad_up, inner_act) for rows_half in halves],
    )
    received = swap(other_share)
    received, feed_terms = lax.optimization_barrier((received, feed_terms))
    pair_two = feed_pair(grad_gate, grad_up, feed_full, received)
    shares_two = [pair_two[0]] + [hop(pair_two[step], "z", -step) for step in (1, 2, 3)]
    feed_sum = lax.psum_scatter(
        feed_terms, "seq", axis_index_groups=planes, scatter_dimension=0, tiled=True
    )
    grad_norm_two = total_of(shares_two)
    upstream = upstream_own.astype(F32)
    grad_resid = upstream + norm_back(grad_norm_two * feed_gain, normal_two, scale_two)
    *grad_attended, _ = gather_rows(grad_resid.astype(BF))

    grad_branch = jnp.concatenate([mm(rows_half, out_full) for rows_half in grad_attended], axis=0)
    grad_switch = (grad_branch * normal_ret * silu_slope(switch)).astype(BF)
    grad_low = norm_back(grad_branch * swish_act, normal_ret, scale_ret).astype(BF)
    grad_onward = (grad_low.astype(F32) * onward).astype(BF)
    early_terms = grads(
        [[(0, 0)], [(1, 1), (2, 2)]],
        [normed_turned, *grad_attended],
        [0],
        [grad_switch, branch[:part], branch[part:]],
        2,
        0,
    )
    outgoing, _ = scan(query, grad_onward, weights[1], where, None)
    grad_scores = (mm(grad_low, value, 1, 1) * within).astype(BF)
    grad_query = mm(grad_scores, key) + mm(grad_onward, incoming, 1, 1)
    grad_key = mm(grad_scores, query, 0, 0) + mm(value, outgoing, 1, 1) * leftover
    grad_value = mm(scores, grad_low, 0, 0) + mm(key_left, outgoing)
    query_grads = turn_back(grad_query).astype(BF)
    key_grads = (turn_back(grad_key) * DK ** (-0.5)).astype(BF)
    qk_grads = jnp.concatenate([query_grads, key_grads], axis=1)
    value_grads = grad_value.astype(BF)

    mixer_terms = grads(
        [[(0, 0)], [(0, 1)]], [normed_turned], [0], [qk_grads, value_grads], 2, 1, early_terms
    )
    mixer_terms, feed_sum = lax.optimization_barrier((mixer_terms, feed_sum))
    mixer_sum = lax.psum_scatter(
        mixer_terms, "seq", axis_index_groups=planes, scatter_dimension=0, tiled=True
    )

    mixer_terms, qk_grads, value_grads, grad_switch, inner_act = lax.optimization_barrier(
        (mixer_terms, qk_grads, value_grads, grad_switch, inner_act)
    )
    feed_own, joint = feed_out_shares(inner_act, feed_full)
    share_own, joint = last_share([qk_grads, value_grads, grad_switch], mixer_full, joint)
    joint_pair = whole(
        pair_body,
        [shaped(F32, half, 2 * model)] + [shaped(BF, half, 2 * model)] * 3,
        z,
        share_own,
        feed_own,
        swap(joint),
    )
    joint_total = total_of(
        [joint_pair[0]] + [hop(joint_pair[step], "z", -step) for step in (1, 2, 3)]
    )
    grad_norm_one = joint_total[:, :model]
    block_output = (residual + joint_total[:, model:]).astype(BF)
    normal_own, scale_own = layer_stats(residual_in)
    tokens_grad = grad_resid + norm_back(grad_norm_one * mixer_gain, normal_own, scale_own)
    norms = jnp.stack(
        [
            jnp.sum(grad_norm_one * normal_own, axis=0),
            jnp.sum(grad_norm_one, axis=0),
            jnp.sum(grad_norm_two * normal_two, axis=0),
            jnp.sum(grad_norm_two, axis=0),
        ]
    )
    norms = norms.reshape(4, SIDE, SIDE, SIDE, -1).transpose(1, 2, 3, 0, 4)
    norms = norms.reshape(SIDE, SIDE, SIDE, -1)
    for axis, dim in (("x", 1), ("y", 0), ("z", 0)):
        norms = reduce_line(norms, axis, dim, where)
    norms = norms.reshape(1, -1)
    norms = (norms + swap(norms)).reshape(4, -1)

    def cut_rows(summed):
        return whole(cut_body, [shaped(BF, shard, summed.shape[1])] * SIDE, z, summed)

    def returned(parts, widths, paired):
        moved = [parts[0]] + [hop(parts[step], "z", step) for step in (1, 2, 3)]
        outs = [shaped(F32, shard, SIDE * width) for width in widths]
        return whole(lambda *refs: unpack_body(paired, *refs), outs, z, *moved)

    gate_sum, up_sum, down_sum = returned(cut_rows(feed_sum), [DV] * 3, ())
    swish_sum, output_sum, query_sum, key_sum, value_sum = returned(
        cut_rows(mixer_sum), [DV, DV, DK, DK, DV], (2, 3)
    )

    def both_halves(values):
        theirs = swap(values)
        return jnp.concatenate(
            [jnp.where(t == 0, values, theirs), jnp.where(t == 0, theirs, values)], axis=0
        )

    return (
        both_halves(block_output),
        both_halves(tokens_grad),
        norms[0],
        norms[1],
        query_sum,
        key_sum,
        value_sum,
        swish_sum,
        output_sum,
        norms[2],
        norms[3],
        gate_sum,
        up_sum,
        down_sum,
    )


def solution(mesh):
    split = P("seq", "tp")
    token = P("seq", None)
    in_specs = (token, P(), P()) + (split,) * 5 + (P(), P()) + (split,) * 3 + (token,)
    out_specs = (token, token, P("seq"), P("seq")) + (split,) * 5 + (P("seq"), P("seq")) + (split,) * 3
    return jax.shard_map(local, mesh=mesh, in_specs=in_specs, out_specs=out_specs, check_vma=False)
```
